32 devices in a mesh: node: 8 (over y, x, core), group: 4 (over z).
Axes of the slice: x: 2, y: 2, z: 4, core: 2. Of those that a mesh axis runs over, the one named last changes fastest.
Arguments:
- tokens: bfloat16 [8192, 1024], P(('node', 'group')), may hold values from -6 to 6
- grad_out: bfloat16 [8192, 1024], P(('node', 'group')), may hold values from -1.5 to 1.5
- router_gate: float32 [8192, 1], P(('node', 'group')), may hold values from 0.1 to 1
- counts: int32 [32], P(('node', 'group')), may hold values from 1 to 2
- routes: int32 [32, 2, 1], P(('node', 'group')), may hold values from 0 to 3, as said below
- partner: int32 [8], replicated, may hold values from 0 to 7, as said below
- w_gate: bfloat16 [32, 1024, 256], P(('node', 'group')), may hold values from -0.1875 to 0.1875
- w_up: bfloat16 [32, 1024, 256], P(('node', 'group')), may hold values from -0.1875 to 0.1875
- w_down: bfloat16 [32, 256, 1024], P(('node', 'group')), may hold values from -0.375 to 0.375
Outputs:
- grad_tokens: bfloat16 [8192, 1024], P(('node', 'group'))
- grad_gate: bfloat16 [32, 1024, 256], P(('node', 'group'))
- grad_up: bfloat16 [32, 1024, 256], P(('node', 'group'))
- grad_down: bfloat16 [32, 256, 1024], P(('node', 'group'))
The draws below stay inside these ranges and needn't reach their ends.
Inputs may be any that keep to these rules, and one draw needn't show every extreme that they name: `routes`: the 2 entries of one device name different devices of its group; every device of a group is named; in every node group one device is named by exactly 3 entries and none by more. partner pairs the nodes: partner[partner[n]] = n and partner[n] != n.
All inputs are finite; a program needn't handle non-finite values.
Results may differ from the reference program's by a relative error of at most 0.015.
Values may be sent and summed in bfloat16 or wider, within the bound.
No kernel may reach another device: no remote copies, remote signals or barrier semaphores. Data moves between devices by JAX's collectives and lax.ppermute only.
A program may use at most 128 MiB of HBM per device.

```python
import math
import jax
import jax.numpy as jnp
from jax import lax

D = 1024
H = 256
BLK = 128
NB = 2
TOPK = 1
MAXR = 3
EXPERTS = 32
ROWS = 8192
N_NODE = 8
N_GROUP = 4


def draw_routes(key, part):
    spread = NB * TOPK
    extra = MAXR - spread
    keys = jax.random.split(key, N_NODE)

    def one_group(subkey):
        first_key, second_key, third_key = jax.random.split(subkey, 3)
        start = jax.random.permutation(first_key, N_GROUP).astype(jnp.int32)
        offsets = jnp.arange(spread, dtype=jnp.int32)
        table = ((start[:, None] + offsets[None, :]) % N_GROUP).astype(jnp.int32)
        hottest = jax.random.randint(second_key, (), 0, N_GROUP).astype(jnp.int32)
        names_hot = jnp.any(table == hottest, axis=1).astype(jnp.int32)
        ranks = jax.random.permutation(third_key, N_GROUP).astype(jnp.int32)
        order = jnp.argsort(names_hot * N_GROUP + ranks).astype(jnp.int32)
        picked = jnp.zeros((N_GROUP,), jnp.int32).at[order[:extra]].set(1)
        final = jnp.where(picked == 1, hottest, table[:, spread - 1]).astype(jnp.int32)
        table = table.at[:, spread - 1].set(final)
        return table.reshape(N_GROUP, NB, TOPK)
    return jax.vmap(one_group)(keys).reshape(N_NODE * N_GROUP, NB, TOPK).astype(jnp.int32)


def draw_partner(key, part):
    order = jax.random.permutation(key, N_NODE).astype(jnp.int32)
    mates = order.reshape(N_NODE // 2, 2)[:, ::-1].reshape(N_NODE)
    return jnp.zeros((N_NODE,), jnp.int32).at[order].set(mates)


def touch_ends(array, key, low, top_value):
    spot = [jax.random.randint(jax.random.fold_in(key, axis), (), 0, length) for axis, length in enumerate(array.shape)]
    main_axis = array.shape.index(max(array.shape))
    next_to = spot[:main_axis] + [(spot[main_axis] + 1) % array.shape[main_axis]] + spot[main_axis + 1:]
    return array.at[tuple(spot)].set(low).at[tuple(next_to)].set(top_value)


def block_scale(own_key, extent, cuts, smallest, high):
    def one(axis_at, shards_of):
        draws = jax.random.uniform(jax.random.fold_in(jax.random.fold_in(own_key, 6), axis_at), (shards_of,), jnp.float32, smallest / len(cuts), high / len(cuts))
        return jnp.repeat(jnp.exp(draws), extent[axis_at] // shards_of).reshape((-1,) + (1,) * (len(extent) - axis_at - 1))

    factor_of = one(*cuts[0])
    for cut in cuts[1:]:
        factor_of = factor_of * one(*cut)
    return factor_of


def bell_draw(key, extent, scale, limit, shards=(), kind=jnp.bfloat16):
    loudness = block_scale(key, extent, shards, -0.22, 0.18) if shards else 1.0
    array = jax.random.normal(key, extent, jnp.float32) * scale * loudness
    return jnp.minimum(jnp.maximum(array, -limit), limit).astype(kind)


def setup_inputs(seed: int = 0) -> dict:
    seeds = jax.random.split(jax.random.key(seed), 10)
    tokens = bell_draw(seeds[0], (ROWS, D), 1.0, 6.0, ((0, 32),))
    grad_out = bell_draw(seeds[1], (ROWS, D), 0.25, 1.5, ((0, 32),))
    router_gate = jnp.clip(jnp.exp(math.log(1.0) - 2.3025851 * jax.random.uniform(seeds[2], (ROWS, TOPK), jnp.float32) ** block_scale(seeds[2], (ROWS, TOPK), ((0, 32),), -0.2, 0.2)), 0.1, 1.0)
    counts = touch_ends(jax.random.randint(seeds[3], (EXPERTS,), 1, NB + 1), jax.random.fold_in(seeds[3], 1), 1, NB).astype(jnp.int32)
    routes = draw_routes(jax.random.fold_in(seeds[9], 71), 0)
    partner = draw_partner(jax.random.fold_in(seeds[9], 71), 0)
    w_gate = bell_draw(seeds[6], (EXPERTS, D, H), D ** -0.5, 0.1875, ((0, 32),))
    w_up = bell_draw(seeds[7], (EXPERTS, D, H), D ** -0.5, 0.1875, ((0, 32),))
    w_down = bell_draw(seeds[8], (EXPERTS, H, D), H ** -0.5, 0.375, ((0, 32),))
    return {"tokens": tokens, "grad_out": grad_out, "router_gate": router_gate, "counts": counts, "routes": routes, "partner": partner, "w_gate": w_gate, "w_up": w_up, "w_down": w_down}


def against(left, right):
    return lax.dot_general(left, right, (((1,), (1,)), ((), ())), preferred_element_type=jnp.float32)


def across(left, right):
    return lax.dot_general(left, right, (((0,), (0,)), ((), ())), preferred_element_type=jnp.float32)


def expert_pass(rows, grads, w_gate, w_up, w_down):
    gate_pre = jnp.dot(rows, w_gate, preferred_element_type=jnp.float32)
    up_pre = jnp.dot(rows, w_up, preferred_element_type=jnp.float32)
    sigmoid = jax.nn.sigmoid(gate_pre)
    swish = gate_pre * sigmoid
    hidden = (swish * up_pre).astype(jnp.bfloat16)
    grad_hidden = against(grads, w_down)
    grad_upre = (grad_hidden * swish).astype(jnp.bfloat16)
    grad_gpre = (grad_hidden * up_pre * sigmoid * (1.0 + gate_pre * (1.0 - sigmoid))).astype(jnp.bfloat16)
    back = (against(grad_gpre, w_gate) + against(grad_upre, w_up)).astype(jnp.bfloat16)
    return (back, across(rows, grad_gpre).astype(jnp.bfloat16),
            across(rows, grad_upre).astype(jnp.bfloat16), across(hidden, grads).astype(jnp.bfloat16))


def reference(tokens, grad_out, router_gate, counts, routes, partner, w_gate, w_up, w_down):
    live = jnp.arange(NB)[None, :] < counts[:, None]
    live_rows = jnp.repeat(live, BLK, axis=1).reshape(ROWS)
    masked_tok = jnp.where(live_rows[:, None], tokens, jnp.zeros_like(tokens))
    masked_out = jnp.where(live_rows[:, None], grad_out, jnp.zeros_like(grad_out))
    tok_nodes = masked_tok.reshape(N_NODE, N_GROUP * NB, BLK, D)
    out_nodes = masked_out.reshape(N_NODE, N_GROUP * NB, BLK, D)
    gate_nodes = router_gate.reshape(N_NODE, N_GROUP * NB, BLK, TOPK)
    route_nodes = routes.reshape(N_NODE, N_GROUP * NB * TOPK)
    placed_gate = jnp.take(w_gate.reshape(N_NODE, N_GROUP, D, H), partner, axis=0)
    placed_up = jnp.take(w_up.reshape(N_NODE, N_GROUP, D, H), partner, axis=0)
    placed_down = jnp.take(w_down.reshape(N_NODE, N_GROUP, H, D), partner, axis=0)

    def per_node(packed):
        tok_g, out_g, gate_g, route_g, wg_g, wu_g, wd_g = packed

        def per_expert(expert, wg, wu, wd):
            chosen = route_g == expert
            index = jnp.argsort(jnp.where(chosen, 0, 1).astype(jnp.int32), stable=True)[:MAXR].astype(jnp.int32)
            valid = chosen[index]
            blocks = (index // TOPK).astype(jnp.int32)
            column = (index % TOPK).astype(jnp.int32)
            keep = valid[:, None, None]
            rows = jnp.where(keep, tok_g[blocks], jnp.zeros((), jnp.bfloat16)).reshape(MAXR * BLK, D)
            weight = gate_g[blocks, :, column]
            grads = (weight[:, :, None] * out_g[blocks].astype(jnp.float32)).astype(jnp.bfloat16)
            grads = jnp.where(keep, grads, jnp.zeros((), jnp.bfloat16)).reshape(MAXR * BLK, D)
            back, grad_wg, grad_wu, grad_wd = expert_pass(rows, grads, wg, wu, wd)
            back = jnp.where(keep, back.reshape(MAXR, BLK, D).astype(jnp.float32), jnp.float32(0.0))
            return back, blocks, grad_wg, grad_wu, grad_wd

        back, blocks, grad_wg, grad_wu, grad_wd = jax.vmap(per_expert)(
            jnp.arange(N_GROUP, dtype=jnp.int32), wg_g, wu_g, wd_g)
        total = jnp.zeros((N_GROUP * NB, BLK, D), jnp.float32).at[blocks.reshape(-1)].add(back.reshape(-1, BLK, D))
        return total.astype(jnp.bfloat16), grad_wg, grad_wu, grad_wd

    back, grad_wg, grad_wu, grad_wd = lax.map(
        per_node, (tok_nodes, out_nodes, gate_nodes, route_nodes, placed_gate, placed_up, placed_down))
    back = back.reshape(ROWS, D)
    grad_tokens = jnp.where(live_rows[:, None], back, jnp.zeros_like(back))
    return (grad_tokens, grad_wg.reshape(EXPERTS, D, H), grad_wu.reshape(EXPERTS, D, H),
            grad_wd.reshape(EXPERTS, H, D))
```

```python
import functools

import jax
import jax.numpy as jnp
from jax import lax
from jax.experimental import pallas as pl
from jax.experimental.pallas import tpu as pltpu
from jax.sharding import PartitionSpec as P

VMEM = pltpu.VMEM
SMEM = pltpu.SMEM
LIMIT = 48 * 1024 * 1024


def dot(left, right, dims):
    return lax.dot_general(left, right, (dims, ((), ())), preferred_element_type=jnp.float32)


def params():
    return pltpu.CompilerParams(vmem_limit_bytes=LIMIT)


def spec(space):
    return pl.BlockSpec(memory_space=space)


def pack_kernel(hops, counts, routes, tokens, grad_out, gate, *places):
    slots, topk = routes.shape[1], routes.shape[2]
    block = tokens.shape[0] // slots
    me = lax.axis_index("group")
    for hop, place in zip(hops, places):
        place[...] = jnp.zeros_like(place)
        for b in range(slots):
            rows = pl.ds(b * block, block)
            for k in range(topk):

                @pl.when((routes[0, b, k] == hop(me)) & (b < counts[0]))
                def _():
                    place[:block] = tokens[rows]
                    scaled = gate[rows, k : k + 1] * grad_out[rows].astype(jnp.float32)
                    place[block:] = scaled.astype(jnp.bfloat16)


def pack(hops, counts, routes, tokens, grad_out, gate):
    slots = routes.shape[1]
    block, depth = tokens.shape[0] // slots, tokens.shape[1]
    place = jax.ShapeDtypeStruct((2 * block, depth), jnp.bfloat16)
    return pl.pallas_call(
        functools.partial(pack_kernel, hops),
        out_shape=[place] * len(hops),
        in_specs=[spec(SMEM), spec(SMEM), spec(VMEM), spec(VMEM), spec(VMEM)],
        out_specs=[spec(VMEM)] * len(hops),
        compiler_params=params(),
        name="pack",
    )(counts, routes, tokens, grad_out, gate)


def expert_kernel(place, w_gate, w_up, w_down, back, inner):
    block = place.shape[0] // 2
    rows, grads = place[:block], place[block:]
    gate_w, up_w = w_gate[...], w_up[...]
    gate_pre = dot(rows, gate_w, ((1,), (0,)))
    up_pre = dot(rows, up_w, ((1,), (0,)))
    sig = 1.0 / (1.0 + jnp.exp(-gate_pre))
    swish = gate_pre * sig
    grad_hidden = dot(grads, w_down[...], ((1,), (1,)))
    grad_upre = (grad_hidden * swish).astype(jnp.bfloat16)
    grad_gpre = (grad_hidden * up_pre * sig * (1.0 + gate_pre * (1.0 - sig))).astype(jnp.bfloat16)
    back[...] = (dot(grad_gpre, gate_w, ((1,), (1,))) + dot(grad_upre, up_w, ((1,), (1,)))).astype(jnp.bfloat16)
    inner[0] = grad_gpre
    inner[1] = grad_upre
    inner[2] = (swish * up_pre).astype(jnp.bfloat16)


def expert(place, w_gate, w_up, w_down):
    block, depth = place.shape[0] // 2, place.shape[1]
    width = w_gate.shape[1]
    return pl.pallas_call(
        expert_kernel,
        out_shape=[
            jax.ShapeDtypeStruct((block, depth), jnp.bfloat16),
            jax.ShapeDtypeStruct((3, block, width), jnp.bfloat16),
        ],
        in_specs=[spec(VMEM)] * 4,
        out_specs=[spec(VMEM)] * 2,
        compiler_params=params(),
        cost_estimate=pl.CostEstimate(
            flops=10 * block * depth * width, bytes_accessed=8 * depth * width, transcendentals=block * width
        ),
        name="expert",
    )(place, w_gate, w_up, w_down)


def weights_kernel(count, *refs):
    places, inners = refs[:count], refs[count : 2 * count]
    grad_gate, grad_up, grad_down = refs[2 * count :]
    block = places[0].shape[0] // 2
    rows = jnp.concatenate([place[:block] for place in places], axis=0)
    grads = jnp.concatenate([place[block:] for place in places], axis=0)
    gpre, upre, hidden = (jnp.concatenate([inner[i] for inner in inners], axis=0) for i in range(3))
    grad_gate[0] = dot(rows, gpre, ((0,), (0,))).astype(jnp.bfloat16)
    grad_up[0] = dot(rows, upre, ((0,), (0,))).astype(jnp.bfloat16)
    grad_down[0] = dot(hidden, grads, ((0,), (0,))).astype(jnp.bfloat16)


def weights(places, inners):
    count = len(places)
    block, depth = places[0].shape[0] // 2, places[0].shape[1]
    width = inners[0].shape[2]
    tile = min(depth, 256)
    wide = jax.ShapeDtypeStruct((1, depth, width), jnp.bfloat16)
    tall = jax.ShapeDtypeStruct((1, width, depth), jnp.bfloat16)
    return pl.pallas_call(
        functools.partial(weights_kernel, count),
        out_shape=[wide, wide, tall],
        grid=(depth // tile,),
        in_specs=[pl.BlockSpec((2 * block, tile), lambda i: (0, i))] * count
        + [pl.BlockSpec((3, block, width), lambda i: (0, 0, 0))] * count,
        out_specs=[
            pl.BlockSpec((1, tile, width), lambda i: (0, i, 0)),
            pl.BlockSpec((1, tile, width), lambda i: (0, i, 0)),
            pl.BlockSpec((1, width, tile), lambda i: (0, 0, i)),
        ],
        compiler_params=params(),
        cost_estimate=pl.CostEstimate(
            flops=6 * count * block * depth * width, bytes_accessed=10 * depth * width, transcendentals=0
        ),
        name="weight_grads",
    )(*places, *inners)


def combine_kernel(hops, counts, routes, *refs):
    returned, out, total = refs[: len(hops)], refs[len(hops)], refs[len(hops) + 1]
    slots, topk = routes.shape[1], routes.shape[2]
    block = out.shape[0] // slots
    me = lax.axis_index("group")
    for b in range(slots):
        total[...] = jnp.zeros_like(total)
        for k in range(topk):
            for hop, part in zip(hops, returned):

                @pl.when((routes[0, b, k] == hop(me)) & (b < counts[0]))
                def _():
                    total[...] += part[...].astype(jnp.float32)

        out[b * block : (b + 1) * block] = total[...].astype(jnp.bfloat16)


def combine(hops, counts, routes, returned):
    slots = routes.shape[1]
    block, depth = returned[0].shape
    return pl.pallas_call(
        functools.partial(combine_kernel, hops),
        out_shape=jax.ShapeDtypeStruct((slots * block, depth), jnp.bfloat16),
        in_specs=[spec(SMEM), spec(SMEM)] + [spec(VMEM)] * len(hops),
        out_specs=spec(VMEM),
        scratch_shapes=[VMEM((block, depth), jnp.float32)],
        compiler_params=params(),
        name="combine",
    )(counts, routes, *returned)


def xor_pairs(size, d):
    return [(i, i ^ d) for i in range(size)]


def relocate(partner, arrays):
    nodes = lax.axis_size("node")
    distance = lax.axis_index("node") ^ partner[lax.axis_index("node")]

    def branch(d):
        return lambda *held: tuple(lax.ppermute(a, "node", xor_pairs(nodes, d)) for a in held)

    return lax.switch(distance - 1, [branch(d) for d in range(1, nodes)], *arrays)


def on_device(tokens, grad_out, router_gate, counts, routes, partner, w_gate, w_up, w_down):
    group = lax.axis_size("group")
    order = sorted(range(1, group), key=lambda d: (d != 2, -d)) + [0]
    hops = [functools.partial(lambda d, me: me ^ d, d) for d in order]
    packed = pack(hops, counts, routes, tokens, grad_out, router_gate)
    places = [
        lax.ppermute(place, "group", xor_pairs(group, d)) if d else place for d, place in zip(order, packed)
    ]
    placed = relocate(partner, (w_gate[0], w_up[0], w_down[0]))
    results = [expert(place, *placed) for place in places]
    returned = [
        lax.ppermute(back, "group", xor_pairs(group, d)) if d else back for d, (back, _) in zip(order, results)
    ]
    grads = weights(places, [inner for _, inner in results])
    grad_tokens = combine(hops, counts, routes, returned)
    return (grad_tokens, *grads)


def solution(mesh):
    both = ("node", "group")
    rows = P(both, None)
    cube = P(both, None, None)
    return jax.shard_map(
        on_device,
        mesh=mesh,
        in_specs=(rows, rows, rows, P(both), cube, P(), cube, cube, cube),
        out_specs=(rows, cube, cube, cube),
        check_vma=False,
    )
```

```python
import functools

import jax
import jax.numpy as jnp
from jax import lax
from jax.experimental import pallas as pl
from jax.experimental.pallas import tpu as pltpu
from jax.sharding import PartitionSpec as P

VMEM = pltpu.VMEM
SMEM = pltpu.SMEM
LIMIT = 48 * 1024 * 1024


def dot(left, right, dims):
    return lax.dot_general(left, right, (dims, ((), ())), preferred_element_type=jnp.float32)


def params():
    return pltpu.CompilerParams(vmem_limit_bytes=LIMIT)


def spec(space):
    return pl.BlockSpec(memory_space=space)


def pack_kernel(hops, counts, routes, tokens, grad_out, gate, *places):
    slots, topk = routes.shape[1], routes.shape[2]
    block = tokens.shape[0] // slots
    me = lax.axis_index("group")
    for hop, place in zip(hops, places):
        place[...] = jnp.zeros_like(place)
        for b in range(slots):
            rows = pl.ds(b * block, block)
            for k in range(topk):

                @pl.when((routes[0, b, k] == hop(me)) & (b < counts[0]))
                def _():
                    place[:block] = tokens[rows]
                    scaled = gate[rows, k : k + 1] * grad_out[rows].astype(jnp.float32)
                    place[block:] = scaled.astype(jnp.bfloat16)


def pack(hops, counts, routes, tokens, grad_out, gate):
    slots = routes.shape[1]
    block, depth = tokens.shape[0] // slots, tokens.shape[1]
    place = jax.ShapeDtypeStruct((2 * block, depth), jnp.bfloat16)
    return pl.pallas_call(
        functools.partial(pack_kernel, hops),
        out_shape=[place] * len(hops),
        in_specs=[spec(SMEM), spec(SMEM), spec(VMEM), spec(VMEM), spec(VMEM)],
        out_specs=[spec(VMEM)] * len(hops),
        compiler_params=params(),
        name="pack",
    )(counts, routes, tokens, grad_out, gate)


def expert_kernel(place, w_gate, w_up, w_down, back, inner):
    block = place.shape[0] // 2
    rows, grads = place[:block], place[block:]
    gate_w, up_w = w_gate[...], w_up[...]
    gate_pre = dot(rows, gate_w, ((1,), (0,)))
    up_pre = dot(rows, up_w, ((1,), (0,)))
    sig = 1.0 / (1.0 + jnp.exp(-gate_pre))
    swish = gate_pre * sig
    grad_hidden = dot(grads, w_down[...], ((1,), (1,)))
    grad_upre = (grad_hidden * swish).astype(jnp.bfloat16)
    grad_gpre = (grad_hidden * up_pre * sig * (1.0 + gate_pre * (1.0 - sig))).astype(jnp.bfloat16)
    back[...] = (dot(grad_gpre, gate_w, ((1,), (1,))) + dot(grad_upre, up_w, ((1,), (1,)))).astype(jnp.bfloat16)
    inner[0] = grad_gpre
    inner[1] = grad_upre
    inner[2] = (swish * up_pre).astype(jnp.bfloat16)


def expert(place, w_gate, w_up, w_down):
    block, depth = place.shape[0] // 2, place.shape[1]
    width = w_gate.shape[1]
    return pl.pallas_call(
        expert_kernel,
        out_shape=[
            jax.ShapeDtypeStruct((block, depth), jnp.bfloat16),
            jax.ShapeDtypeStruct((3, block, width), jnp.bfloat16),
        ],
        in_specs=[spec(VMEM)] * 4,
        out_specs=[spec(VMEM)] * 2,
        compiler_params=params(),
        cost_estimate=pl.CostEstimate(
            flops=10 * block * depth * width, bytes_accessed=8 * depth * width, transcendentals=block * width
        ),
        name="expert",
    )(place, w_gate, w_up, w_down)


def weights_kernel(count, *refs):
    places, inners = refs[:count], refs[count : 2 * count]
    grad_gate, grad_up, grad_down = refs[2 * count :]
    block = places[0].shape[0] // 2
    rows = jnp.concatenate([place[:block] for place in places], axis=0)
    grads = jnp.concatenate([place[block:] for place in places], axis=0)
    gpre, upre, hidden = (jnp.concatenate([inner[i] for inner in inners], axis=0) for i in range(3))
    grad_gate[0] = dot(rows, gpre, ((0,), (0,))).astype(jnp.bfloat16)
    grad_up[0] = dot(rows, upre, ((0,), (0,))).astype(jnp.bfloat16)
    grad_down[0] = dot(hidden, grads, ((0,), (0,))).astype(jnp.bfloat16)


def weights(places, inners):
    count = len(places)
    block, depth = places[0].shape[0] // 2, places[0].shape[1]
    width = inners[0].shape[2]
    tile = min(depth, 256)
    wide = jax.ShapeDtypeStruct((1, depth, width), jnp.bfloat16)
    tall = jax.ShapeDtypeStruct((1, width, depth), jnp.bfloat16)
    return pl.pallas_call(
        functools.partial(weights_kernel, count),
        out_shape=[wide, wide, tall],
        grid=(depth // tile,),
        in_specs=[pl.BlockSpec((2 * block, tile), lambda i: (0, i))] * count
        + [pl.BlockSpec((3, block, width), lambda i: (0, 0, 0))] * count,
        out_specs=[
            pl.BlockSpec((1, tile, width), lambda i: (0, i, 0)),
            pl.BlockSpec((1, tile, width), lambda i: (0, i, 0)),
            pl.BlockSpec((1, width, tile), lambda i: (0, 0, i)),
        ],
        compiler_params=params(),
        cost_estimate=pl.CostEstimate(
            flops=6 * count * block * depth * width, bytes_accessed=10 * depth * width, transcendentals=0
        ),
        name="weight_grads",
    )(*places, *inners)


def combine_kernel(hops, counts, routes, *refs):
    returned, out, total = refs[: len(hops)], refs[len(hops)], refs[len(hops) + 1]
    slots, topk = routes.shape[1], routes.shape[2]
    block = out.shape[0] // slots
    me = lax.axis_index("group")
    for b in range(slots):
        total[...] = jnp.zeros_like(total)
        for k in range(topk):
            for hop, part in zip(hops, returned):

                @pl.when((routes[0, b, k] == hop(me)) & (b < counts[0]))
                def _():
                    total[...] += part[...].astype(jnp.float32)

        out[b * block : (b + 1) * block] = total[...].astype(jnp.bfloat16)


def combine(hops, counts, routes, returned):
    slots = routes.shape[1]
    block, depth = returned[0].shape
    return pl.pallas_call(
        functools.partial(combine_kernel, hops),
        out_shape=jax.ShapeDtypeStruct((slots * block, depth), jnp.bfloat16),
        in_specs=[spec(SMEM), spec(SMEM)] + [spec(VMEM)] * len(hops),
        out_specs=spec(VMEM),
        scratch_shapes=[VMEM((block, depth), jnp.float32)],
        compiler_params=params(),
        name="combine",
    )(counts, routes, *returned)


def xor_pairs(size, d):
    return [(i, i ^ d) for i in range(size)]


def pass_at(d, counts, routes, tokens, grad_out, gate, w_gate, w_up, w_down):
    nodes, group = lax.axis_size("node"), lax.axis_size("group")
    placed = [lax.ppermute(w, "node", xor_pairs(nodes, d)) if d else w for w in (w_gate, w_up, w_down)]
    order = sorted(range(1, group), key=lambda d: (d != 2, -d)) + [0]
    hops = [functools.partial(lambda d, me: me ^ d, d) for d in order]
    packed = pack(hops, counts, routes, tokens, grad_out, gate)
    places = [
        lax.ppermute(place, "group", xor_pairs(group, d)) if d else place for d, place in zip(order, packed)
    ]
    results = [expert(place, *placed) for place in places]
    returned = [
        lax.ppermute(back, "group", xor_pairs(group, d)) if d else back for d, (back, _) in zip(order, results)
    ]
    grads = weights(places, [inner for _, inner in results])
    grad_tokens = combine(hops, counts, routes, returned)
    return (grad_tokens, *grads)


def relocate(nodes, distance, arrays):
    def branch(d):
        return lambda *held: tuple(lax.ppermute(a, "node", xor_pairs(nodes, d)) for a in held)

    return lax.switch(distance - 1, [branch(d) for d in range(1, nodes)], *arrays)


def on_device(tokens, grad_out, router_gate, counts, routes, partner, w_gate, w_up, w_down):
    nodes = lax.axis_size("node")
    distance = lax.axis_index("node") ^ partner[lax.axis_index("node")]
    rows = (counts, routes, tokens, grad_out, router_gate)
    held = (w_gate[0], w_up[0], w_down[0])
    if nodes > 8:
        return pass_at(0, *rows, *relocate(nodes, distance, held))
    branches = [functools.partial(pass_at, d) for d in range(1, nodes)]
    return lax.switch(distance - 1, branches, *rows, *held)


def solution(mesh):
    both = ("node", "group")
    rows = P(both, None)
    cube = P(both, None, None)
    return jax.shard_map(
        on_device,
        mesh=mesh,
        in_specs=(rows, rows, rows, P(both), cube, P(), cube, cube, cube),
        out_specs=(rows, cube, cube, cube),
        check_vma=False,
    )
```

```python
import functools

import jax
import jax.numpy as jnp
from jax import lax
from jax.experimental import pallas as pl
from jax.experimental.pallas import tpu as pltpu
from jax.sharding import PartitionSpec as P

VMEM = pltpu.VMEM
SMEM = pltpu.SMEM
LIMIT = 48 * 1024 * 1024


def dot(left, right, dims):
    return lax.dot_general(left, right, (dims, ((), ())), preferred_element_type=jnp.float32)


def params():
    return pltpu.CompilerParams(vmem_limit_bytes=LIMIT)


def in_hbm(array):
    return pltpu.with_memory_space_constraint(array, pltpu.HBM)


def spec(space):
    return pl.BlockSpec(memory_space=space)


def pack_kernel(hops, shape, counts, partner, routes, tokens, grad_out, gate, w_gate, w_up, w_down, *refs):
    slots, topk = shape
    places, (stack, plan, goals) = refs[: len(hops)], refs[len(hops) : len(hops) + 3]
    partner_s, routes_s, grads_v, gate_v, sems, place_sems, stack_sems = refs[len(hops) + 3 :]
    depth, width = w_gate.shape[1:]
    squares = depth // width
    first = [
        pltpu.make_async_copy(routes, routes_s, sems.at[0]),
        pltpu.make_async_copy(partner, partner_s, sems.at[1]),
        pltpu.make_async_copy(gate, gate_v, sems.at[2]),
        pltpu.make_async_copy(grad_out, grads_v, sems.at[3]),
    ]
    stacked = [
        pltpu.make_async_copy(w_gate.at[0], stack.at[pl.ds(0, depth)], stack_sems.at[0]),
        pltpu.make_async_copy(w_up.at[0], stack.at[pl.ds(depth, depth)], stack_sems.at[1]),
    ] + [
        pltpu.make_async_copy(
            w_down.at[0, :, pl.ds(i * width, width)],
            stack.at[pl.ds(2 * depth + i * width, width)],
            stack_sems.at[2 + i],
        )
        for i in range(squares)
    ]
    for copy in first + stacked:
        copy.start()
    block = grads_v.shape[0] // slots
    me, node = lax.axis_index("group"), lax.axis_index("node")
    first[0].wait()
    entries = [(b, k) for b in range(slots) for k in range(topk)]
    sent = [[(routes_s[b * topk + k] == hop(me)) & (b < counts[0]) for b, k in entries] for hop in hops]

    def tokens_to(place, b, i):
        return pltpu.make_async_copy(tokens.at[pl.ds(b * block, block)], place.at[pl.ds(0, block)], place_sems.at[i])

    for i, place in enumerate(places):
        for (b, k), found in zip(entries, sent[i]):

            @pl.when(found)
            def _():
                tokens_to(place, b, i).start()

    for i, place in enumerate(places):

        @pl.when(jnp.logical_not(functools.reduce(jnp.logical_or, sent[i])))
        def _():
            place[...] = jnp.zeros_like(place)

    for copy in first[1:]:
        copy.wait()
    plan[0] = (node ^ partner_s[node]) - 1
    for i, (b, _) in enumerate(entries):
        goals[i] = jnp.where(b < counts[0], routes_s[i], -1)
    for i, place in enumerate(places):
        for (b, k), found in zip(entries, sent[i]):

            @pl.when(found)
            def _():
                rows = pl.ds(b * block, block)
                scaled = gate_v[k : k + 1, rows].T * grads_v[rows].astype(jnp.float32)
                place[block:] = scaled.astype(jnp.bfloat16)

    for i, place in enumerate(places):
        for (b, k), found in zip(entries, sent[i]):

            @pl.when(found)
            def _():
                tokens_to(place, b, i).wait()

    for copy in stacked:
        copy.wait()


def pack(hops, partner, counts, routes, tokens, grad_out, gate, w_gate, w_up, w_down):
    slots, topk = routes.shape[1], routes.shape[2]
    length, depth = tokens.shape
    width = w_gate.shape[2]
    place = jax.ShapeDtypeStruct((2 * length // slots, depth), jnp.bfloat16)
    *places, stack, plan, goals = pl.pallas_call(
        functools.partial(pack_kernel, hops, (slots, topk)),
        out_shape=[place] * len(hops)
        + [jax.ShapeDtypeStruct((3 * depth, width), jnp.bfloat16)]
        + [SMEM((1,), jnp.int32), SMEM((slots * topk,), jnp.int32)],
        in_specs=[spec(SMEM)] + [spec(pltpu.HBM)] * 8,
        out_specs=[spec(VMEM)] * (len(hops) + 1) + [spec(SMEM)] * 2,
        scratch_shapes=[
            SMEM(partner.shape, jnp.int32),
            SMEM((slots * topk,), jnp.int32),
            VMEM((length, depth), jnp.bfloat16),
            VMEM((topk, length), jnp.float32),
            pltpu.SemaphoreType.DMA((4,)),
            pltpu.SemaphoreType.DMA((len(hops),)),
            pltpu.SemaphoreType.DMA((2 + depth // width,)),
        ],
        compiler_params=params(),
        name="pack",
    )(counts, *map(in_hbm, (partner, routes.reshape(slots * topk), tokens, grad_out, gate.T, w_gate, w_up, w_down)))
    return places, stack, plan, goals


def expert_kernel(place, stack, back, inner):
    block, depth = place.shape[0] // 2, place.shape[1]
    width = stack.shape[1]
    rows, grads = place[:block], place[block:]
    gate_w, up_w = stack[:depth], stack[depth : 2 * depth]
    gate_pre = dot(rows, gate_w, ((1,), (0,)))
    up_pre = dot(rows, up_w, ((1,), (0,)))
    sig = 1.0 / (1.0 + jnp.exp(-gate_pre))
    swish = gate_pre * sig
    grad_hidden = jnp.zeros_like(gate_pre)
    for i in range(0, depth, width):
        square = stack[2 * depth + i : 2 * depth + i + width]
        grad_hidden += dot(grads[:, i : i + width], square, ((1,), (1,)))
    grad_upre = (grad_hidden * swish).astype(jnp.bfloat16)
    grad_gpre = (grad_hidden * up_pre * sig * (1.0 + gate_pre * (1.0 - sig))).astype(jnp.bfloat16)
    back[...] = (dot(grad_gpre, gate_w, ((1,), (1,))) + dot(grad_upre, up_w, ((1,), (1,)))).astype(jnp.bfloat16)
    inner[0] = grad_gpre
    inner[1] = grad_upre
    inner[2] = (swish * up_pre).astype(jnp.bfloat16)


def expert(place, stack):
    block, depth = place.shape[0] // 2, place.shape[1]
    width = stack.shape[1]
    return pl.pallas_call(
        expert_kernel,
        out_shape=[
            jax.ShapeDtypeStruct((block, depth), jnp.bfloat16),
            jax.ShapeDtypeStruct((3, block, width), jnp.bfloat16),
        ],
        in_specs=[spec(VMEM)] * 2,
        out_specs=[spec(VMEM)] * 2,
        compiler_params=params(),
        cost_estimate=pl.CostEstimate(
            flops=10 * block * depth * width, bytes_accessed=8 * depth * width, transcendentals=block * width
        ),
        name="expert",
    )(place, stack)


def weights_kernel(count, *refs):
    places, inners = refs[:count], refs[count : 2 * count]
    grad_gate, grad_up, grad_down = refs[2 * count :]
    block = places[0].shape[0] // 2
    rows = jnp.concatenate([place[:block] for place in places], axis=0)
    grads = jnp.concatenate([place[block:] for place in places], axis=0)
    gpre, upre, hidden = (jnp.concatenate([inner[i] for inner in inners], axis=0) for i in range(3))
    grad_gate[0] = dot(rows, gpre, ((0,), (0,))).astype(jnp.bfloat16)
    grad_up[0] = dot(rows, upre, ((0,), (0,))).astype(jnp.bfloat16)
    grad_down[0] = dot(hidden, grads, ((0,), (0,))).astype(jnp.bfloat16)


def weights(places, inners):
    count = len(places)
    block, depth = places[0].shape[0] // 2, places[0].shape[1]
    width = inners[0].shape[2]
    tile = min(depth, 256)
    wide = jax.ShapeDtypeStruct((1, depth, width), jnp.bfloat16)
    tall = jax.ShapeDtypeStruct((1, width, depth), jnp.bfloat16)
    return pl.pallas_call(
        functools.partial(weights_kernel, count),
        out_shape=[wide, wide, tall],
        grid=(depth // tile,),
        in_specs=[pl.BlockSpec((2 * block, tile), lambda i: (0, i))] * count
        + [pl.BlockSpec((3, block, width), lambda i: (0, 0, 0))] * count,
        out_specs=[
            pl.BlockSpec((1, tile, width), lambda i: (0, i, 0)),
            pl.BlockSpec((1, tile, width), lambda i: (0, i, 0)),
            pl.BlockSpec((1, width, tile), lambda i: (0, 0, i)),
        ],
        compiler_params=params(),
        cost_estimate=pl.CostEstimate(
            flops=6 * count * block * depth * width, bytes_accessed=10 * depth * width, transcendentals=0
        ),
        name="weight_grads",
    )(*places, *inners)


def settle_kernel(hops, shape, goals, *refs):
    returned, out, empty, sems = refs[: len(hops)], refs[len(hops)], refs[len(hops) + 1], refs[len(hops) + 2]
    slots = shape[0]
    block = empty.shape[0]
    me = lax.axis_index("group")
    empty[...] = jnp.zeros_like(empty)
    for b in range(slots):
        target = out.at[pl.ds(b * block, block)]
        for hop, part in zip(hops, returned):

            @pl.when(goals[b] == hop(me))
            def _():
                pltpu.make_async_copy(part, target, sems.at[b]).start()

        @pl.when(goals[b] < 0)
        def _():
            pltpu.make_async_copy(empty, target, sems.at[b]).start()

    for b in range(slots):
        pltpu.make_async_copy(empty, out.at[pl.ds(b * block, block)], sems.at[b]).wait()


def combine_kernel(hops, shape, goals, *refs):
    returned, out, total = refs[: len(hops)], refs[len(hops)], refs[len(hops) + 1]
    slots, topk = shape
    block = out.shape[0] // slots
    me = lax.axis_index("group")
    for b in range(slots):
        total[...] = jnp.zeros_like(total)
        for k in range(topk):
            for hop, part in zip(hops, returned):

                @pl.when(goals[b * topk + k] == hop(me))
                def _():
                    total[...] += part[...].astype(jnp.float32)

        out[b * block : (b + 1) * block] = total[...].astype(jnp.bfloat16)


def combine(hops, shape, goals, returned):
    slots, topk = shape
    block, depth = returned[0].shape
    if topk == 1:
        kernel, where_from, where_to = settle_kernel, pl.ANY, pltpu.HBM
        scratch = [VMEM((block, depth), jnp.bfloat16), pltpu.SemaphoreType.DMA((slots,))]
    else:
        kernel, where_from, where_to = combine_kernel, VMEM, VMEM
        scratch = [VMEM((block, depth), jnp.float32)]
    return pl.pallas_call(
        functools.partial(kernel, hops, (slots, topk)),
        out_shape=where_to((slots * block, depth), jnp.bfloat16),
        in_specs=[spec(SMEM)] + [spec(where_from)] * len(hops),
        out_specs=spec(where_to),
        scratch_shapes=scratch,
        compiler_params=params(),
        name="combine",
    )(goals, *returned)


def xor_pairs(size, d):
    return [(i, i ^ d) for i in range(size)]


def pass_at(d, order, hops, shape, goals, stack, *packed):
    nodes, group = lax.axis_size("node"), lax.axis_size("group")
    stack = lax.ppermute(stack, "node", xor_pairs(nodes, d)) if d else stack
    places = [
        lax.ppermute(place, "group", xor_pairs(group, d)) if d else place for d, place in zip(order, packed)
    ]
    results = []
    for place in places:
        results.append(expert(place, stack))
        stack, _ = lax.optimization_barrier((stack, results[-1][1]))
    returned = [
        lax.ppermute(back, "group", xor_pairs(group, d)) if d else back for d, (back, _) in zip(order, results)
    ]
    grads = weights(places, [inner for _, inner in results])
    grad_tokens = combine(hops, shape, goals, returned)
    return (grad_tokens, *grads)


def on_device(tokens, grad_out, router_gate, counts, routes, partner, w_gate, w_up, w_down):
    nodes, group = lax.axis_size("node"), lax.axis_size("group")
    shape = routes.shape[1:]
    order = sorted(range(1, group), key=lambda d: (d != 2, -d)) + [0]
    hops = [functools.partial(lambda d, me: me ^ d, d) for d in order]
    packed, stack, plan, goals = pack(hops, partner, counts, routes, tokens, grad_out, router_gate, w_gate, w_up, w_down)
    if nodes > 8:
        moves = [
            functools.partial(lax.ppermute, axis_name="node", perm=xor_pairs(nodes, d)) for d in range(1, nodes)
        ]
        return pass_at(0, order, hops, shape, goals, lax.switch(plan[0], moves, stack), *packed)
    branches = [functools.partial(pass_at, d, order, hops, shape) for d in range(1, nodes)]
    return lax.switch(plan[0], branches, goals, stack, *packed)


def solution(mesh):
    both = ("node", "group")
    rows = P(both, None)
    cube = P(both, None, None)
    return jax.shard_map(
        on_device,
        mesh=mesh,
        in_specs=(rows, rows, rows, P(both), cube, P(), cube, cube, cube),
        out_specs=(rows, cube, cube, cube),
        check_vma=False,
    )
```

```python
import functools

import jax
import jax.numpy as jnp
from jax import lax
from jax.experimental import pallas as pl
from jax.experimental.pallas import tpu as pltpu
from jax.sharding import PartitionSpec as P

VMEM = pltpu.VMEM
SMEM = pltpu.SMEM
LIMIT = 48 * 1024 * 1024


def dot(left, right, dims):
    return lax.dot_general(left, right, (dims, ((), ())), preferred_element_type=jnp.float32)


def params():
    return pltpu.CompilerParams(vmem_limit_bytes=LIMIT)


def in_hbm(array):
    return pltpu.with_memory_space_constraint(array, pltpu.HBM)


def spec(space):
    return pl.BlockSpec(memory_space=space)


EMPTY = 64.0


def pack_kernel(hops, shape, counts, partner, routes, tokens, grad_out, gate, w_gate, w_up, w_down, *refs):
    slots, topk = shape
    places, (stack, plan, goals) = refs[: len(hops)], refs[len(hops) : len(hops) + 3]
    partner_s, routes_s, grads_v, gate_v, sems, place_sems, stack_sems = refs[len(hops) + 3 :]
    depth, width = w_gate.shape[1:]
    squares = depth // width
    first = [
        pltpu.make_async_copy(routes, routes_s, sems.at[0]),
        pltpu.make_async_copy(partner, partner_s, sems.at[1]),
        pltpu.make_async_copy(gate, gate_v, sems.at[2]),
        pltpu.make_async_copy(grad_out, grads_v, sems.at[3]),
    ]
    stacked = [
        pltpu.make_async_copy(w_gate.at[0], stack.at[pl.ds(0, depth)], stack_sems.at[0]),
        pltpu.make_async_copy(w_up.at[0], stack.at[pl.ds(depth, depth)], stack_sems.at[1]),
    ] + [
        pltpu.make_async_copy(
            w_down.at[0, :, pl.ds(i * width, width)],
            stack.at[pl.ds(2 * depth + i * width, width)],
            stack_sems.at[2 + i],
        )
        for i in range(squares)
    ]
    for copy in first + stacked:
        copy.start()
    block = grads_v.shape[0] // slots
    me, node = lax.axis_index("group"), lax.axis_index("node")
    first[0].wait()
    entries = [(b, k) for b in range(slots) for k in range(topk)]
    sent = [[(routes_s[b * topk + k] == hop(me)) & (b < counts[0]) for b, k in entries] for hop in hops]

    def tokens_to(place, b, i):
        return pltpu.make_async_copy(tokens.at[pl.ds(b * block, block)], place.at[pl.ds(0, block)], place_sems.at[i])

    for i, place in enumerate(places):
        for (b, k), found in zip(entries, sent[i]):

            @pl.when(found)
            def _():
                tokens_to(place, b, i).start()

    for i, place in enumerate(places):

        @pl.when(jnp.logical_not(functools.reduce(jnp.logical_or, sent[i])))
        def _():
            place[...] = jnp.full(place.shape, EMPTY, place.dtype)

    for copy in first[1:]:
        copy.wait()
    plan[0] = (node ^ partner_s[node]) - 1
    for i, (b, _) in enumerate(entries):
        goals[i] = jnp.where(b < counts[0], routes_s[i], -1)
    for i, place in enumerate(places):
        for (b, k), found in zip(entries, sent[i]):

            @pl.when(found)
            def _():
                rows = pl.ds(b * block, block)
                scaled = gate_v[k : k + 1, rows].T * grads_v[rows].astype(jnp.float32)
                place[block:] = scaled.astype(jnp.bfloat16)

    for i, place in enumerate(places):
        for (b, k), found in zip(entries, sent[i]):

            @pl.when(found)
            def _():
                tokens_to(place, b, i).wait()

    for copy in stacked:
        copy.wait()


def pack(hops, partner, counts, routes, tokens, grad_out, gate, w_gate, w_up, w_down):
    slots, topk = routes.shape[1], routes.shape[2]
    length, depth = tokens.shape
    width = w_gate.shape[2]
    place = jax.ShapeDtypeStruct((2 * length // slots, depth), jnp.bfloat16)
    *places, stack, plan, goals = pl.pallas_call(
        functools.partial(pack_kernel, hops, (slots, topk)),
        out_shape=[place] * len(hops)
        + [jax.ShapeDtypeStruct((3 * depth, width), jnp.bfloat16)]
        + [SMEM((1,), jnp.int32), SMEM((slots * topk,), jnp.int32)],
        in_specs=[spec(SMEM)] + [spec(pltpu.HBM)] * 8,
        out_specs=[spec(VMEM)] * (len(hops) + 1) + [spec(SMEM)] * 2,
        scratch_shapes=[
            SMEM(partner.shape, jnp.int32),
            SMEM((slots * topk,), jnp.int32),
            VMEM((length, depth), jnp.bfloat16),
            VMEM((topk, length), jnp.float32),
            pltpu.SemaphoreType.DMA((4,)),
            pltpu.SemaphoreType.DMA((len(hops),)),
            pltpu.SemaphoreType.DMA((2 + depth // width,)),
        ],
        compiler_params=params(),
        name="pack",
    )(counts, *map(in_hbm, (partner, routes.reshape(slots * topk), tokens, grad_out, gate.T, w_gate, w_up, w_down)))
    return places, stack, plan, goals


def expert_pass(place, stack, back, inner):
    block, depth = place.shape[0] // 2, place.shape[1]
    width = stack.shape[1]
    rows, grads = place[:block], place[block:]
    gate_w, up_w = stack[:depth], stack[depth : 2 * depth]
    gate_pre = dot(rows, gate_w, ((1,), (0,)))
    up_pre = dot(rows, up_w, ((1,), (0,)))
    sig = 1.0 / (1.0 + jnp.exp(-gate_pre))
    swish = gate_pre * sig
    grad_hidden = jnp.zeros_like(gate_pre)
    for i in range(0, depth, width):
        square = stack[2 * depth + i : 2 * depth + i + width]
        grad_hidden += dot(grads[:, i : i + width], square, ((1,), (1,)))
    grad_upre = (grad_hidden * swish).astype(jnp.bfloat16)
    grad_gpre = (grad_hidden * up_pre * sig * (1.0 + gate_pre * (1.0 - sig))).astype(jnp.bfloat16)
    back[...] = (dot(grad_gpre, gate_w, ((1,), (1,))) + dot(grad_upre, up_w, ((1,), (1,)))).astype(jnp.bfloat16)
    inner[0] = grad_gpre
    inner[1] = grad_upre
    inner[2] = (swish * up_pre).astype(jnp.bfloat16)


def expert_kernel(d, place, goals, stack, back, inner, case):
    me = lax.axis_index("group")
    lower = (me ^ d) > me
    full = jnp.max(place[:16, :128].astype(jnp.float32)) < EMPTY / 2
    sent = functools.reduce(jnp.logical_or, [goals[i] == (me ^ d) for i in range(goals.shape[0])])
    case[0] = jnp.where(full, jnp.where(lower, 1, 2), 0) + jnp.where(sent, jnp.where(lower, 2, 1), 0)

    @pl.when(full)
    def _():
        expert_pass(place, stack, back, inner)

    @pl.when(jnp.logical_not(full))
    def _():
        back[...] = jnp.zeros_like(back)
        inner[...] = jnp.zeros_like(inner)


def expert(d, place, goals, stack):
    block, depth = place.shape[0] // 2, place.shape[1]
    width = stack.shape[1]
    return pl.pallas_call(
        functools.partial(expert_kernel, d),
        out_shape=[
            jax.ShapeDtypeStruct((block, depth), jnp.bfloat16),
            jax.ShapeDtypeStruct((3, block, width), jnp.bfloat16),
            SMEM((1,), jnp.int32),
        ],
        in_specs=[spec(VMEM), spec(SMEM), spec(VMEM)],
        out_specs=[spec(VMEM), spec(VMEM), spec(SMEM)],
        compiler_params=params(),
        cost_estimate=pl.CostEstimate(
            flops=10 * block * depth * width, bytes_accessed=8 * depth * width, transcendentals=block * width
        ),
        name="expert",
    )(place, goals, stack)


def weights_kernel(count, *refs):
    places, inners = refs[:count], refs[count : 2 * count]
    grad_gate, grad_up, grad_down = refs[2 * count :]
    block = places[0].shape[0] // 2
    rows = jnp.concatenate([place[:block] for place in places], axis=0)
    grads = jnp.concatenate([place[block:] for place in places], axis=0)
    gpre, upre, hidden = (jnp.concatenate([inner[i] for inner in inners], axis=0) for i in range(3))
    grad_gate[0] = dot(rows, gpre, ((0,), (0,))).astype(jnp.bfloat16)
    grad_up[0] = dot(rows, upre, ((0,), (0,))).astype(jnp.bfloat16)
    grad_down[0] = dot(hidden, grads, ((0,), (0,))).astype(jnp.bfloat16)


def weights(places, inners):
    count = len(places)
    block, depth = places[0].shape[0] // 2, places[0].shape[1]
    width = inners[0].shape[2]
    tile = min(depth, 256)
    wide = jax.ShapeDtypeStruct((1, depth, width), jnp.bfloat16)
    tall = jax.ShapeDtypeStruct((1, width, depth), jnp.bfloat16)
    return pl.pallas_call(
        functools.partial(weights_kernel, count),
        out_shape=[wide, wide, tall],
        grid=(depth // tile,),
        in_specs=[pl.BlockSpec((2 * block, tile), lambda i: (0, i))] * count
        + [pl.BlockSpec((3, block, width), lambda i: (0, 0, 0))] * count,
        out_specs=[
            pl.BlockSpec((1, tile, width), lambda i: (0, i, 0)),
            pl.BlockSpec((1, tile, width), lambda i: (0, i, 0)),
            pl.BlockSpec((1, width, tile), lambda i: (0, 0, i)),
        ],
        compiler_params=params(),
        cost_estimate=pl.CostEstimate(
            flops=6 * count * block * depth * width, bytes_accessed=10 * depth * width, transcendentals=0
        ),
        name="weight_grads",
    )(*places, *inners)


def settle_kernel(hops, shape, goals, *refs):
    returned, out, empty, sems = refs[: len(hops)], refs[len(hops)], refs[len(hops) + 1], refs[len(hops) + 2]
    slots = shape[0]
    block = empty.shape[0]
    me = lax.axis_index("group")
    empty[...] = jnp.zeros_like(empty)
    for b in range(slots):
        target = out.at[pl.ds(b * block, block)]
        for hop, part in zip(hops, returned):

            @pl.when(goals[b] == hop(me))
            def _():
                pltpu.make_async_copy(part, target, sems.at[b]).start()

        @pl.when(goals[b] < 0)
        def _():
            pltpu.make_async_copy(empty, target, sems.at[b]).start()

    for b in range(slots):
        pltpu.make_async_copy(empty, out.at[pl.ds(b * block, block)], sems.at[b]).wait()


def combine_kernel(hops, shape, goals, *refs):
    returned, out, total = refs[: len(hops)], refs[len(hops)], refs[len(hops) + 1]
    slots, topk = shape
    block = out.shape[0] // slots
    me = lax.axis_index("group")
    for b in range(slots):
        total[...] = jnp.zeros_like(total)
        for k in range(topk):
            for hop, part in zip(hops, returned):

                @pl.when(goals[b * topk + k] == hop(me))
                def _():
                    total[...] += part[...].astype(jnp.float32)

        out[b * block : (b + 1) * block] = total[...].astype(jnp.bfloat16)


def combine(hops, shape, goals, returned):
    slots, topk = shape
    block, depth = returned[0].shape
    if topk == 1:
        kernel, where_from, where_to = settle_kernel, pl.ANY, pltpu.HBM
        scratch = [VMEM((block, depth), jnp.bfloat16), pltpu.SemaphoreType.DMA((slots,))]
    else:
        kernel, where_from, where_to = combine_kernel, VMEM, VMEM
        scratch = [VMEM((block, depth), jnp.float32)]
    return pl.pallas_call(
        functools.partial(kernel, hops, (slots, topk)),
        out_shape=where_to((slots * block, depth), jnp.bfloat16),
        in_specs=[spec(SMEM)] + [spec(where_from)] * len(hops),
        out_specs=spec(where_to),
        scratch_shapes=scratch,
        compiler_params=params(),
        name="combine",
    )(goals, *returned)


def xor_pairs(size, d):
    return [(i, i ^ d) for i in range(size)]


def to_xor(array, d, axis="group"):
    return lax.ppermute(array, axis, xor_pairs(lax.axis_size(axis), d))


def after(array, *others):
    return lax.optimization_barrier((array, *others))[0]


def give_back(case, back, d, beside=lambda: ()):
    pairs = xor_pairs(lax.axis_size("group"), d)
    up = [(a, b) for a, b in pairs if a < b]
    down = [(a, b) for a, b in pairs if a > b]

    def branch(perm):
        return lambda array: (lax.ppermute(array, "group", perm) if perm else array, beside())

    return lax.switch(case[0], [branch(perm) for perm in ([], up, down, pairs)], back)


def on_device(tokens, grad_out, router_gate, counts, routes, partner, w_gate, w_up, w_down):
    nodes, group = lax.axis_size("node"), lax.axis_size("group")
    shape = routes.shape[1:]
    order = sorted(range(1, group), key=lambda d: (d != 2, -d)) + [0]
    optional = (2, 3) if group == 4 else ()
    hops = [functools.partial(lambda d, me: me ^ d, d) for d in order]
    packed, stack, plan, goals = pack(hops, partner, counts, routes, tokens, grad_out, router_gate, w_gate, w_up, w_down)
    places = {d: to_xor(place, d) if d else place for d, place in zip(order, packed)}
    moves = [functools.partial(to_xor, d=d, axis="node") for d in range(1, nodes)]
    stack = lax.switch(plan[0], moves, stack)
    inners, returned = {}, {}
    turns = sorted(order, key=lambda d: (d in optional, d))
    for d in turns:
        back, inners[d], case = expert(d, places[d], goals, stack)
        stack = after(stack, inners[d])
        if d == 0 or d not in optional:
            returned[d] = to_xor(back, d) if d else back
        elif d == optional[0]:
            returned[d], _ = give_back(case, back, d)
            stack = after(stack, returned[d])
        else:
            beside = lambda: weights([places[d] for d in order], [inners[d] for d in order])
            returned[d], grads = give_back(case, back, d, beside)
    if len(optional) < 2:
        grads = weights([places[d] for d in order], [inners[d] for d in order])
    return (combine(hops, shape, goals, [returned[d] for d in order]), *grads)


def solution(mesh):
    both = ("node", "group")
    rows = P(both, None)
    cube = P(both, None, None)
    return jax.shard_map(
        on_device,
        mesh=mesh,
        in_specs=(rows, rows, rows, P(both), cube, P(), cube, cube, cube),
        out_specs=(rows, cube, cube, cube),
        check_vma=False,
    )
```

```python
import functools

import jax
import jax.numpy as jnp
from jax import lax
from jax.experimental import pallas as pl
from jax.experimental.pallas import tpu as pltpu
from jax.sharding import PartitionSpec as P

VMEM = pltpu.VMEM
SMEM = pltpu.SMEM
LIMIT = 48 * 1024 * 1024


def dot(left, right, dims):
    return lax.dot_general(left, right, (dims, ((), ())), preferred_element_type=jnp.float32)


def params():
    return pltpu.CompilerParams(vmem_limit_bytes=LIMIT)


def in_hbm(array):
    return pltpu.with_memory_space_constraint(array, pltpu.HBM)


def spec(space):
    return pl.BlockSpec(memory_space=space)


EMPTY = 64.0


def pack_kernel(hops, shape, counts, partner, routes, tokens, grad_out, gate, w_gate, w_up, w_down, *refs):
    slots, topk = shape
    places, (stack, plan, goals) = refs[: len(hops)], refs[len(hops) : len(hops) + 3]
    partner_s, routes_s, grads_v, gate_v, sems, place_sems, stack_sems = refs[len(hops) + 3 :]
    depth, width = w_gate.shape[1:]
    squares = depth // width
    first = [
        pltpu.make_async_copy(routes, routes_s, sems.at[0]),
        pltpu.make_async_copy(partner, partner_s, sems.at[1]),
        pltpu.make_async_copy(gate, gate_v, sems.at[2]),
        pltpu.make_async_copy(grad_out, grads_v, sems.at[3]),
    ]
    stacked = [
        pltpu.make_async_copy(w_gate.at[0], stack.at[pl.ds(0, depth)], stack_sems.at[0]),
        pltpu.make_async_copy(w_up.at[0], stack.at[pl.ds(depth, depth)], stack_sems.at[1]),
    ] + [
        pltpu.make_async_copy(
            w_down.at[0, :, pl.ds(i * width, width)],
            stack.at[pl.ds(2 * depth + i * width, width)],
            stack_sems.at[2 + i],
        )
        for i in range(squares)
    ]
    for copy in first + stacked:
        copy.start()
    block = grads_v.shape[0] // slots
    me, node = lax.axis_index("group"), lax.axis_index("node")
    first[0].wait()
    entries = [(b, k) for b in range(slots) for k in range(topk)]
    sent = [[(routes_s[b * topk + k] == hop(me)) & (b < counts[0]) for b, k in entries] for hop in hops]

    def tokens_to(place, b, i):
        return pltpu.make_async_copy(tokens.at[pl.ds(b * block, block)], place.at[pl.ds(0, block)], place_sems.at[i])

    for i, place in enumerate(places):
        for (b, k), found in zip(entries, sent[i]):

            @pl.when(found)
            def _():
                tokens_to(place, b, i).start()

    for i, place in enumerate(places):

        @pl.when(jnp.logical_not(functools.reduce(jnp.logical_or, sent[i])))
        def _():
            place[...] = jnp.full(place.shape, EMPTY, place.dtype)

    for copy in first[1:]:
        copy.wait()
    plan[0] = (node ^ partner_s[node]) - 1
    for i, (b, _) in enumerate(entries):
        goals[i] = jnp.where(b < counts[0], routes_s[i], -1)
    for i, place in enumerate(places):
        for (b, k), found in zip(entries, sent[i]):

            @pl.when(found)
            def _():
                rows = pl.ds(b * block, block)
                scaled = gate_v[k : k + 1, rows].T * grads_v[rows].astype(jnp.float32)
                place[block:] = scaled.astype(jnp.bfloat16)

    for i, place in enumerate(places):
        for (b, k), found in zip(entries, sent[i]):

            @pl.when(found)
            def _():
                tokens_to(place, b, i).wait()

    for copy in stacked:
        copy.wait()


def pack(hops, partner, counts, routes, tokens, grad_out, gate, w_gate, w_up, w_down):
    slots, topk = routes.shape[1], routes.shape[2]
    length, depth = tokens.shape
    width = w_gate.shape[2]
    place = jax.ShapeDtypeStruct((2 * length // slots, depth), jnp.bfloat16)
    *places, stack, plan, goals = pl.pallas_call(
        functools.partial(pack_kernel, hops, (slots, topk)),
        out_shape=[place] * len(hops)
        + [jax.ShapeDtypeStruct((3 * depth, width), jnp.bfloat16)]
        + [SMEM((1,), jnp.int32), SMEM((slots * topk,), jnp.int32)],
        in_specs=[spec(SMEM)] + [spec(pltpu.HBM)] * 8,
        out_specs=[spec(VMEM)] * (len(hops) + 1) + [spec(SMEM)] * 2,
        scratch_shapes=[
            SMEM(partner.shape, jnp.int32),
            SMEM((slots * topk,), jnp.int32),
            VMEM((length, depth), jnp.bfloat16),
            VMEM((topk, length), jnp.float32),
            pltpu.SemaphoreType.DMA((4,)),
            pltpu.SemaphoreType.DMA((len(hops),)),
            pltpu.SemaphoreType.DMA((2 + depth // width,)),
        ],
        compiler_params=params(),
        name="pack",
    )(counts, *map(in_hbm, (partner, routes.reshape(slots * topk), tokens, grad_out, gate.T, w_gate, w_up, w_down)))
    return places, stack, plan, goals


def expert_pass(place, stack, back, inner):
    block, depth = place.shape[0] // 2, place.shape[1]
    width = stack.shape[1]
    rows, grads = place[:block], place[block:]
    gate_w, up_w = stack[:depth], stack[depth : 2 * depth]
    gate_pre = dot(rows, gate_w, ((1,), (0,)))
    up_pre = dot(rows, up_w, ((1,), (0,)))
    sig = 1.0 / (1.0 + jnp.exp(-gate_pre))
    swish = gate_pre * sig
    grad_hidden = jnp.zeros_like(gate_pre)
    for i in range(0, depth, width):
        square = stack[2 * depth + i : 2 * depth + i + width]
        grad_hidden += dot(grads[:, i : i + width], square, ((1,), (1,)))
    grad_upre = (grad_hidden * swish).astype(jnp.bfloat16)
    grad_gpre = (grad_hidden * up_pre * sig * (1.0 + gate_pre * (1.0 - sig))).astype(jnp.bfloat16)
    back[...] = (dot(grad_gpre, gate_w, ((1,), (1,))) + dot(grad_upre, up_w, ((1,), (1,)))).astype(jnp.bfloat16)
    inner[0] = grad_gpre
    inner[1] = grad_upre
    inner[2] = (swish * up_pre).astype(jnp.bfloat16)


def expert_kernel(d, place, goals, stack, back, inner, case):
    me = lax.axis_index("group")
    lower = (me ^ d) > me
    full = jnp.max(place[:16, :128].astype(jnp.float32)) < EMPTY / 2
    sent = functools.reduce(jnp.logical_or, [goals[i] == (me ^ d) for i in range(goals.shape[0])])
    case[0] = jnp.where(full, jnp.where(lower, 1, 2), 0) + jnp.where(sent, jnp.where(lower, 2, 1), 0)

    @pl.when(full)
    def _():
        expert_pass(place, stack, back, inner)

    @pl.when(jnp.logical_not(full))
    def _():
        back[...] = jnp.zeros_like(back)
        inner[...] = jnp.zeros_like(inner)


def load_kernel(array, out, sem):
    copy = pltpu.make_async_copy(array, out, sem)
    copy.start()
    copy.wait()


def load(array):
    return pl.pallas_call(
        load_kernel,
        out_shape=VMEM(array.shape, array.dtype),
        in_specs=[spec(pl.ANY)],
        out_specs=spec(VMEM),
        scratch_shapes=[pltpu.SemaphoreType.DMA],
        compiler_params=params(),
        name="load",
    )(array)


def expert(d, place, goals, stack):
    block, depth = place.shape[0] // 2, place.shape[1]
    width = stack.shape[1]
    return pl.pallas_call(
        functools.partial(expert_kernel, d),
        out_shape=[
            jax.ShapeDtypeStruct((block, depth), jnp.bfloat16),
            jax.ShapeDtypeStruct((3, block, width), jnp.bfloat16),
            SMEM((1,), jnp.int32),
        ],
        in_specs=[spec(VMEM), spec(SMEM), spec(VMEM)],
        out_specs=[spec(VMEM), spec(VMEM), spec(SMEM)],
        compiler_params=params(),
        cost_estimate=pl.CostEstimate(
            flops=10 * block * depth * width, bytes_accessed=8 * depth * width, transcendentals=block * width
        ),
        name="expert",
    )(place, goals, stack)


def weights_kernel(count, *refs):
    places, inners = refs[:count], refs[count : 2 * count]
    grad_gate, grad_up, grad_down = refs[2 * count :]
    block = places[0].shape[0] // 2
    rows = jnp.concatenate([place[:block] for place in places], axis=0)
    grads = jnp.concatenate([place[block:] for place in places], axis=0)
    gpre, upre, hidden = (jnp.concatenate([inner[i] for inner in inners], axis=0) for i in range(3))
    grad_gate[0] = dot(rows, gpre, ((0,), (0,))).astype(jnp.bfloat16)
    grad_up[0] = dot(rows, upre, ((0,), (0,))).astype(jnp.bfloat16)
    grad_down[0] = dot(hidden, grads, ((0,), (0,))).astype(jnp.bfloat16)


def weights(places, inners):
    count = len(places)
    block, depth = places[0].shape[0] // 2, places[0].shape[1]
    width = inners[0].shape[2]
    tile = min(depth, 256)
    wide = jax.ShapeDtypeStruct((1, depth, width), jnp.bfloat16)
    tall = jax.ShapeDtypeStruct((1, width, depth), jnp.bfloat16)
    return pl.pallas_call(
        functools.partial(weights_kernel, count),
        out_shape=[wide, wide, tall],
        grid=(depth // tile,),
        in_specs=[pl.BlockSpec((2 * block, tile), lambda i: (0, i))] * count
        + [pl.BlockSpec((3, block, width), lambda i: (0, 0, 0))] * count,
        out_specs=[
            pl.BlockSpec((1, tile, width), lambda i: (0, i, 0)),
            pl.BlockSpec((1, tile, width), lambda i: (0, i, 0)),
            pl.BlockSpec((1, width, tile), lambda i: (0, 0, i)),
        ],
        compiler_params=params(),
        cost_estimate=pl.CostEstimate(
            flops=6 * count * block * depth * width, bytes_accessed=10 * depth * width, transcendentals=0
        ),
        name="weight_grads",
    )(*places, *inners)


def settle_kernel(hops, shape, goals, *refs):
    returned, out, empty, sems = refs[: len(hops)], refs[len(hops)], refs[len(hops) + 1], refs[len(hops) + 2]
    slots = shape[0]
    block = empty.shape[0]
    me = lax.axis_index("group")
    empty[...] = jnp.zeros_like(empty)
    for b in range(slots):
        target = out.at[pl.ds(b * block, block)]
        for hop, part in zip(hops, returned):

            @pl.when(goals[b] == hop(me))
            def _():
                pltpu.make_async_copy(part, target, sems.at[b]).start()

        @pl.when(goals[b] < 0)
        def _():
            pltpu.make_async_copy(empty, target, sems.at[b]).start()

    for b in range(slots):
        pltpu.make_async_copy(empty, out.at[pl.ds(b * block, block)], sems.at[b]).wait()


def combine_kernel(hops, shape, goals, *refs):
    returned, out, total = refs[: len(hops)], refs[len(hops)], refs[len(hops) + 1]
    slots, topk = shape
    block = out.shape[0] // slots
    me = lax.axis_index("group")
    for b in range(slots):
        total[...] = jnp.zeros_like(total)
        for k in range(topk):
            for hop, part in zip(hops, returned):

                @pl.when(goals[b * topk + k] == hop(me))
                def _():
                    total[...] += part[...].astype(jnp.float32)

        out[b * block : (b + 1) * block] = total[...].astype(jnp.bfloat16)


def combine(hops, shape, goals, returned):
    slots, topk = shape
    block, depth = returned[0].shape
    if topk == 1:
        kernel, where_from, where_to = settle_kernel, pl.ANY, pltpu.HBM
        scratch = [VMEM((block, depth), jnp.bfloat16), pltpu.SemaphoreType.DMA((slots,))]
    else:
        kernel, where_from, where_to = combine_kernel, VMEM, VMEM
        scratch = [VMEM((block, depth), jnp.float32)]
    return pl.pallas_call(
        functools.partial(kernel, hops, (slots, topk)),
        out_shape=where_to((slots * block, depth), jnp.bfloat16),
        in_specs=[spec(SMEM)] + [spec(where_from)] * len(hops),
        out_specs=spec(where_to),
        scratch_shapes=scratch,
        compiler_params=params(),
        name="combine",
    )(goals, *returned)


def xor_pairs(size, d):
    return [(i, i ^ d) for i in range(size)]


def to_xor(array, d, axis="group"):
    return lax.ppermute(array, axis, xor_pairs(lax.axis_size(axis), d))


def after(array, *others):
    return lax.optimization_barrier((array, *others))[0]


def give_back(case, back, d, beside=lambda: ()):
    pairs = xor_pairs(lax.axis_size("group"), d)
    up = [(a, b) for a, b in pairs if a < b]
    down = [(a, b) for a, b in pairs if a > b]

    def branch(perm):
        return lambda array: (lax.ppermute(array, "group", perm) if perm else array, beside())

    return lax.switch(case[0], [branch(perm) for perm in ([], up, down, pairs)], back)


def on_device(tokens, grad_out, router_gate, counts, routes, partner, w_gate, w_up, w_down):
    nodes, group = lax.axis_size("node"), lax.axis_size("group")
    shape = routes.shape[1:]
    order = sorted(range(1, group), key=lambda d: (d != 2, -d)) + [0]
    optional = (3,) if group == 4 else ()
    hops = [functools.partial(lambda d, me: me ^ d, d) for d in order]
    packed, stack, plan, goals = pack(hops, partner, counts, routes, tokens, grad_out, router_gate, w_gate, w_up, w_down)
    places = {d: to_xor(place, d) if d else place for d, place in zip(order, packed)}
    moves = [functools.partial(to_xor, d=d, axis="node") for d in range(1, nodes)]
    stack = load(lax.switch(plan[0], moves, stack))
    inners, returned = {}, {}
    turns = [d for d in (2, 1, 0) if d < group] + list(range(3, group))
    for d in turns:
        back, inners[d], case = expert(d, places[d], goals, stack)
        stack = after(stack, inners[d])
        if d == 0 or d not in optional:
            returned[d] = to_xor(back, d) if d else back
        elif d != optional[-1]:
            returned[d], _ = give_back(case, back, d)
            stack = after(stack, returned[d])
        else:
            beside = lambda: weights([places[d] for d in order], [inners[d] for d in order])
            returned[d], grads = give_back(case, back, d, beside)
    if not optional:
        grads = weights([places[d] for d in order], [inners[d] for d in order])
    return (combine(hops, shape, goals, [returned[d] for d in order]), *grads)


def solution(mesh):
    both = ("node", "group")
    rows = P(both, None)
    cube = P(both, None, None)
    return jax.shard_map(
        on_device,
        mesh=mesh,
        in_specs=(rows, rows, rows, P(both), cube, P(), cube, cube, cube),
        out_specs=(rows, cube, cube, cube),
        check_vma=False,
    )
```

```python
import functools

import jax
import jax.numpy as jnp
from jax import lax
from jax.experimental import pallas as pl
from jax.experimental.pallas import tpu as pltpu
from jax.sharding import PartitionSpec as P

VMEM = pltpu.VMEM
SMEM = pltpu.SMEM
LIMIT = 48 * 1024 * 1024


def dot(left, right, dims):
    return lax.dot_general(left, right, (dims, ((), ())), preferred_element_type=jnp.float32)


def params():
    return pltpu.CompilerParams(vmem_limit_bytes=LIMIT)


def in_hbm(array):
    return pltpu.with_memory_space_constraint(array, pltpu.HBM)


def spec(space):
    return pl.BlockSpec(memory_space=space)


EMPTY = 64.0


def pack_kernel(hops, shape, counts, partner, routes, tokens, grad_out, gate, w_gate, w_up, w_down, *refs):
    slots, topk = shape
    places, (stack, plan, goals) = refs[: len(hops)], refs[len(hops) : len(hops) + 3]
    partner_s, routes_s, grads_v, gate_v, sems, place_sems, stack_sems = refs[len(hops) + 3 :]
    depth, width = w_gate.shape[1:]
    squares = depth // width
    first = [
        pltpu.make_async_copy(routes, routes_s, sems.at[0]),
        pltpu.make_async_copy(partner, partner_s, sems.at[1]),
        pltpu.make_async_copy(gate, gate_v, sems.at[2]),
        pltpu.make_async_copy(grad_out, grads_v, sems.at[3]),
    ]
    stacked = [
        pltpu.make_async_copy(w_gate.at[0], stack.at[pl.ds(0, depth)], stack_sems.at[0]),
        pltpu.make_async_copy(w_up.at[0], stack.at[pl.ds(depth, depth)], stack_sems.at[1]),
    ] + [
        pltpu.make_async_copy(
            w_down.at[0, :, pl.ds(i * width, width)],
            stack.at[pl.ds(2 * depth + i * width, width)],
            stack_sems.at[2 + i],
        )
        for i in range(squares)
    ]
    for copy in first + stacked:
        copy.start()
    block = grads_v.shape[0] // slots
    me, node = lax.axis_index("group"), lax.axis_index("node")
    first[0].wait()
    entries = [(b, k) for b in range(slots) for k in range(topk)]
    sent = [[(routes_s[b * topk + k] == hop(me)) & (b < counts[0]) for b, k in entries] for hop in hops]

    def tokens_to(place, b, i):
        return pltpu.make_async_copy(tokens.at[pl.ds(b * block, block)], place.at[pl.ds(0, block)], place_sems.at[i])

    for i, place in enumerate(places):
        for (b, k), found in zip(entries, sent[i]):

            @pl.when(found)
            def _():
                tokens_to(place, b, i).start()

    for i, place in enumerate(places):

        @pl.when(jnp.logical_not(functools.reduce(jnp.logical_or, sent[i])))
        def _():
            place[...] = jnp.full(place.shape, EMPTY, place.dtype)

    for copy in first[1:]:
        copy.wait()
    plan[0] = (node ^ partner_s[node]) - 1
    for i, (b, _) in enumerate(entries):
        goals[i] = jnp.where(b < counts[0], routes_s[i], -1)
    for i, place in enumerate(places):
        for (b, k), found in zip(entries, sent[i]):

            @pl.when(found)
            def _():
                rows = pl.ds(b * block, block)
                scaled = gate_v[k : k + 1, rows].T * grads_v[rows].astype(jnp.float32)
                place[block:] = scaled.astype(jnp.bfloat16)

    for i, place in enumerate(places):
        for (b, k), found in zip(entries, sent[i]):

            @pl.when(found)
            def _():
                tokens_to(place, b, i).wait()

    for copy in stacked:
        copy.wait()


def pack(hops, partner, counts, routes, tokens, grad_out, gate, w_gate, w_up, w_down):
    slots, topk = routes.shape[1], routes.shape[2]
    length, depth = tokens.shape
    width = w_gate.shape[2]
    place = jax.ShapeDtypeStruct((2 * length // slots, depth), jnp.bfloat16)
    *places, stack, plan, goals = pl.pallas_call(
        functools.partial(pack_kernel, hops, (slots, topk)),
        out_shape=[place] * len(hops)
        + [jax.ShapeDtypeStruct((3 * depth, width), jnp.bfloat16)]
        + [SMEM((1,), jnp.int32), SMEM((slots * topk,), jnp.int32)],
        in_specs=[spec(SMEM)] + [spec(pltpu.HBM)] * 8,
        out_specs=[spec(VMEM)] * (len(hops) + 1) + [spec(SMEM)] * 2,
        scratch_shapes=[
            SMEM(partner.shape, jnp.int32),
            SMEM((slots * topk,), jnp.int32),
            VMEM((length, depth), jnp.bfloat16),
            VMEM((topk, length), jnp.float32),
            pltpu.SemaphoreType.DMA((4,)),
            pltpu.SemaphoreType.DMA((len(hops),)),
            pltpu.SemaphoreType.DMA((2 + depth // width,)),
        ],
        compiler_params=params(),
        name="pack",
    )(counts, *map(in_hbm, (partner, routes.reshape(slots * topk), tokens, grad_out, gate.T, w_gate, w_up, w_down)))
    return places, stack, plan, goals


def expert_pass(place, stack, back, inner):
    block, depth = place.shape[0] // 2, place.shape[1]
    width = stack.shape[1]
    rows, grads = place[:block], place[block:]
    gate_w, up_w = stack[:depth], stack[depth : 2 * depth]
    gate_pre = dot(rows, gate_w, ((1,), (0,)))
    up_pre = dot(rows, up_w, ((1,), (0,)))
    sig = 1.0 / (1.0 + jnp.exp(-gate_pre))
    swish = gate_pre * sig
    grad_hidden = jnp.zeros_like(gate_pre)
    for i in range(0, depth, width):
        square = stack[2 * depth + i : 2 * depth + i + width]
        grad_hidden += dot(grads[:, i : i + width], square, ((1,), (1,)))
    grad_upre = (grad_hidden * swish).astype(jnp.bfloat16)
    grad_gpre = (grad_hidden * up_pre * sig * (1.0 + gate_pre * (1.0 - sig))).astype(jnp.bfloat16)
    back[...] = (dot(grad_gpre, gate_w, ((1,), (1,))) + dot(grad_upre, up_w, ((1,), (1,)))).astype(jnp.bfloat16)
    inner[0] = grad_gpre
    inner[1] = grad_upre
    inner[2] = (swish * up_pre).astype(jnp.bfloat16)


def expert_kernel(d, place, goals, stack, back, inner, case):
    me = lax.axis_index("group")
    lower = (me ^ d) > me
    full = jnp.max(place[:16, :128].astype(jnp.float32)) < EMPTY / 2
    sent = functools.reduce(jnp.logical_or, [goals[i] == (me ^ d) for i in range(goals.shape[0])])
    case[0] = jnp.where(full, jnp.where(lower, 1, 2), 0) + jnp.where(sent, jnp.where(lower, 2, 1), 0)

    @pl.when(full)
    def _():
        expert_pass(place, stack, back, inner)

    @pl.when(jnp.logical_not(full))
    def _():
        back[...] = jnp.zeros_like(back)
        inner[...] = jnp.zeros_like(inner)


def load_kernel(array, out, sem):
    copy = pltpu.make_async_copy(array, out, sem)
    copy.start()
    copy.wait()


def load(array):
    return pl.pallas_call(
        load_kernel,
        out_shape=VMEM(array.shape, array.dtype),
        in_specs=[spec(pl.ANY)],
        out_specs=spec(VMEM),
        scratch_shapes=[pltpu.SemaphoreType.DMA],
        compiler_params=params(),
        name="load",
    )(array)


def expert(d, place, goals, stack):
    block, depth = place.shape[0] // 2, place.shape[1]
    width = stack.shape[1]
    return pl.pallas_call(
        functools.partial(expert_kernel, d),
        out_shape=[
            jax.ShapeDtypeStruct((block, depth), jnp.bfloat16),
            jax.ShapeDtypeStruct((3, block, width), jnp.bfloat16),
            SMEM((1,), jnp.int32),
        ],
        in_specs=[spec(VMEM), spec(SMEM), spec(VMEM)],
        out_specs=[spec(VMEM), spec(VMEM), spec(SMEM)],
        compiler_params=params(),
        cost_estimate=pl.CostEstimate(
            flops=10 * block * depth * width, bytes_accessed=8 * depth * width, transcendentals=block * width
        ),
        name="expert",
    )(place, goals, stack)


def weights_kernel(count, *refs):
    places, inners = refs[:count], refs[count : 2 * count]
    grad_gate, grad_up, grad_down = refs[2 * count :]
    block = places[0].shape[0] // 2
    rows = jnp.concatenate([place[:block] for place in places], axis=0)
    grads = jnp.concatenate([place[block:] for place in places], axis=0)
    gpre, upre, hidden = (jnp.concatenate([inner[i] for inner in inners], axis=0) for i in range(3))
    grad_gate[0] = dot(rows, gpre, ((0,), (0,))).astype(jnp.bfloat16)
    grad_up[0] = dot(rows, upre, ((0,), (0,))).astype(jnp.bfloat16)
    grad_down[0] = dot(hidden, grads, ((0,), (0,))).astype(jnp.bfloat16)


def weights(places, inners):
    count = len(places)
    block, depth = places[0].shape[0] // 2, places[0].shape[1]
    width = inners[0].shape[2]
    tile = min(depth, 256)
    wide = jax.ShapeDtypeStruct((1, depth, width), jnp.bfloat16)
    tall = jax.ShapeDtypeStruct((1, width, depth), jnp.bfloat16)
    return pl.pallas_call(
        functools.partial(weights_kernel, count),
        out_shape=[wide, wide, tall],
        grid=(depth // tile,),
        in_specs=[pl.BlockSpec((2 * block, tile), lambda i: (0, i))] * count
        + [pl.BlockSpec((3, block, width), lambda i: (0, 0, 0))] * count,
        out_specs=[
            pl.BlockSpec((1, tile, width), lambda i: (0, i, 0)),
            pl.BlockSpec((1, tile, width), lambda i: (0, i, 0)),
            pl.BlockSpec((1, width, tile), lambda i: (0, 0, i)),
        ],
        compiler_params=params(),
        cost_estimate=pl.CostEstimate(
            flops=6 * count * block * depth * width, bytes_accessed=10 * depth * width, transcendentals=0
        ),
        name="weight_grads",
    )(*places, *inners)


def settle_kernel(hops, shape, goals, *refs):
    returned, out, empty, sems = refs[: len(hops)], refs[len(hops)], refs[len(hops) + 1], refs[len(hops) + 2]
    slots = shape[0]
    block = empty.shape[0]
    me = lax.axis_index("group")
    empty[...] = jnp.zeros_like(empty)
    for b in range(slots):
        target = out.at[pl.ds(b * block, block)]
        for hop, part in zip(hops, returned):

            @pl.when(goals[b] == hop(me))
            def _():
                pltpu.make_async_copy(part, target, sems.at[b]).start()

        @pl.when(goals[b] < 0)
        def _():
            pltpu.make_async_copy(empty, target, sems.at[b]).start()

    for b in range(slots):
        pltpu.make_async_copy(empty, out.at[pl.ds(b * block, block)], sems.at[b]).wait()


def combine_kernel(hops, shape, goals, *refs):
    returned, out, total = refs[: len(hops)], refs[len(hops)], refs[len(hops) + 1]
    slots, topk = shape
    block = out.shape[0] // slots
    me = lax.axis_index("group")
    for b in range(slots):
        total[...] = jnp.zeros_like(total)
        for k in range(topk):
            for hop, part in zip(hops, returned):

                @pl.when(goals[b * topk + k] == hop(me))
                def _():
                    total[...] += part[...].astype(jnp.float32)

        out[b * block : (b + 1) * block] = total[...].astype(jnp.bfloat16)


def combine(hops, shape, goals, returned):
    slots, topk = shape
    block, depth = returned[0].shape
    if topk == 1:
        kernel, where_from, where_to = settle_kernel, pl.ANY, pltpu.HBM
        scratch = [VMEM((block, depth), jnp.bfloat16), pltpu.SemaphoreType.DMA((slots,))]
    else:
        kernel, where_from, where_to = combine_kernel, VMEM, VMEM
        scratch = [VMEM((block, depth), jnp.float32)]
    return pl.pallas_call(
        functools.partial(kernel, hops, (slots, topk)),
        out_shape=where_to((slots * block, depth), jnp.bfloat16),
        in_specs=[spec(SMEM)] + [spec(where_from)] * len(hops),
        out_specs=spec(where_to),
        scratch_shapes=scratch,
        compiler_params=params(),
        name="combine",
    )(goals, *returned)


def xor_pairs(size, d):
    return [(i, i ^ d) for i in range(size)]


def to_xor(array, d, axis="group"):
    return lax.ppermute(array, axis, xor_pairs(lax.axis_size(axis), d))


def after(array, *others):
    return lax.optimization_barrier((array, *others))[0]


def give_back(case, back, d, beside=lambda: ()):
    pairs = xor_pairs(lax.axis_size("group"), d)
    up = [(a, b) for a, b in pairs if a < b]
    down = [(a, b) for a, b in pairs if a > b]

    def branch(perm):
        return lambda array: (lax.ppermute(array, "group", perm) if perm else array, beside())

    return lax.switch(case[0], [branch(perm) for perm in ([], up, down, pairs)], back)


def on_device(tokens, grad_out, router_gate, counts, routes, partner, w_gate, w_up, w_down):
    nodes, group = lax.axis_size("node"), lax.axis_size("group")
    shape = routes.shape[1:]
    order = sorted(range(1, group), key=lambda d: (d != 3, -d)) + [0]
    optional = (2,) if group == 4 else ()
    hops = [functools.partial(lambda d, me: me ^ d, d) for d in order]
    packed, stack, plan, goals = pack(hops, partner, counts, routes, tokens, grad_out, router_gate, w_gate, w_up, w_down)
    places = {d: to_xor(place, d) if d else place for d, place in zip(order, packed)}
    moves = [functools.partial(to_xor, d=d, axis="node") for d in range(1, nodes)]
    stack = load(lax.switch(plan[0], moves, stack))
    inners, returned = {}, {}
    turns = [d for d in (3, 1, 0) if d < group] + [2] + list(range(4, group))
    for d in turns:
        back, inners[d], case = expert(d, places[d], goals, stack)
        stack = after(stack, inners[d])
        if d == 0 or d not in optional:
            returned[d] = to_xor(back, d) if d else back
        elif d != optional[-1]:
            returned[d], _ = give_back(case, back, d)
            stack = after(stack, returned[d])
        else:
            beside = lambda: weights([places[d] for d in order], [inners[d] for d in order])
            returned[d], grads = give_back(case, back, d, beside)
    if not optional:
        grads = weights([places[d] for d in order], [inners[d] for d in order])
    return (combine(hops, shape, goals, [returned[d] for d in order]), *grads)


def solution(mesh):
    both = ("node", "group")
    rows = P(both, None)
    cube = P(both, None, None)
    return jax.shard_map(
        on_device,
        mesh=mesh,
        in_specs=(rows, rows, rows, P(both), cube, P(), cube, cube, cube),
        out_specs=(rows, cube, cube, cube),
        check_vma=False,
    )
```

```python
import functools

import jax
import jax.numpy as jnp
from jax import lax
from jax.experimental import pallas as pl
from jax.experimental.pallas import tpu as pltpu
from jax.sharding import PartitionSpec as P

VMEM = pltpu.VMEM
SMEM = pltpu.SMEM
LIMIT = 48 * 1024 * 1024


def dot(left, right, dims):
    return lax.dot_general(left, right, (dims, ((), ())), preferred_element_type=jnp.float32)


def params():
    return pltpu.CompilerParams(vmem_limit_bytes=LIMIT)


def in_hbm(array):
    return pltpu.with_memory_space_constraint(array, pltpu.HBM)


def spec(space):
    return pl.BlockSpec(memory_space=space)


EMPTY = 64.0


def pack_kernel(hops, shape, counts, partner, routes, tokens, grad_out, gate, *refs):
    slots, topk = shape
    places, (plan, goals) = refs[: len(hops)], refs[len(hops) : len(hops) + 2]
    partner_s, routes_s, tokens_v, grads_v, gate_v, sems = refs[len(hops) + 2 :]
    copies = [
        pltpu.make_async_copy(source, target, sems.at[i])
        for i, (source, target) in enumerate(
            [(routes, routes_s), (partner, partner_s), (gate, gate_v), (grad_out, grads_v), (tokens, tokens_v)]
        )
    ]
    for copy in copies:
        copy.start()
    block = grads_v.shape[0] // slots
    me, node = lax.axis_index("group"), lax.axis_index("node")
    copies[0].wait()
    entries = [(b, k) for b in range(slots) for k in range(topk)]
    sent = [[(routes_s[b * topk + k] == hop(me)) & (b < counts[0]) for b, k in entries] for hop in hops]
    for i, place in enumerate(places):

        @pl.when(jnp.logical_not(functools.reduce(jnp.logical_or, sent[i])))
        def _():
            place[...] = jnp.full(place.shape, EMPTY, place.dtype)

    for copy in copies[1:]:
        copy.wait()
    plan[0] = (node ^ partner_s[node]) - 1
    for i, (b, _) in enumerate(entries):
        goals[i] = jnp.where(b < counts[0], routes_s[i], -1)
    for i, place in enumerate(places):
        for (b, k), found in zip(entries, sent[i]):

            @pl.when(found)
            def _():
                rows = pl.ds(b * block, block)
                scaled = gate_v[k : k + 1, rows].T * grads_v[rows].astype(jnp.float32)
                place[:block] = tokens_v[rows]
                place[block:] = scaled.astype(jnp.bfloat16)


def pack(hops, partner, counts, routes, tokens, grad_out, gate):
    slots, topk = routes.shape[1], routes.shape[2]
    length, depth = tokens.shape
    place = jax.ShapeDtypeStruct((2 * length // slots, depth), jnp.bfloat16)
    *places, plan, goals = pl.pallas_call(
        functools.partial(pack_kernel, hops, (slots, topk)),
        out_shape=[place] * len(hops) + [SMEM((1,), jnp.int32), SMEM((slots * topk,), jnp.int32)],
        in_specs=[spec(SMEM)] + [spec(pltpu.HBM)] * 5,
        out_specs=[spec(VMEM)] * len(hops) + [spec(SMEM)] * 2,
        scratch_shapes=[
            SMEM(partner.shape, jnp.int32),
            SMEM((slots * topk,), jnp.int32),
            VMEM((length, depth), jnp.bfloat16),
            VMEM((length, depth), jnp.bfloat16),
            VMEM((topk, length), jnp.float32),
            pltpu.SemaphoreType.DMA((5,)),
        ],
        compiler_params=params(),
        name="pack",
    )(counts, *map(in_hbm, (partner, routes.reshape(slots * topk), tokens, grad_out, gate.T)))
    return places, plan, goals


def stack_kernel(w_gate, w_up, w_down, stack, sems):
    depth, width = w_gate.shape[1:]
    copies = [
        pltpu.make_async_copy(w_gate.at[0], stack.at[pl.ds(0, depth)], sems.at[0]),
        pltpu.make_async_copy(w_up.at[0], stack.at[pl.ds(depth, depth)], sems.at[1]),
    ] + [
        pltpu.make_async_copy(
            w_down.at[0, :, pl.ds(i * width, width)],
            stack.at[pl.ds(2 * depth + i * width, width)],
            sems.at[2 + i],
        )
        for i in range(depth // width)
    ]
    for copy in copies:
        copy.start()
    for copy in copies:
        copy.wait()


def stacked(w_gate, w_up, w_down):
    depth, width = w_gate.shape[1:]
    return pl.pallas_call(
        stack_kernel,
        out_shape=jax.ShapeDtypeStruct((3 * depth, width), jnp.bfloat16),
        in_specs=[spec(pltpu.HBM)] * 3,
        out_specs=spec(VMEM),
        scratch_shapes=[pltpu.SemaphoreType.DMA((2 + depth // width,))],
        compiler_params=params(),
        name="stack",
    )(*map(in_hbm, (w_gate, w_up, w_down)))


def expert_pass(place, stack, back, inner):
    block, depth = place.shape[0] // 2, place.shape[1]
    width = stack.shape[1]
    rows, grads = place[:block], place[block:]
    gate_w, up_w = stack[:depth], stack[depth : 2 * depth]
    gate_pre = dot(rows, gate_w, ((1,), (0,)))
    up_pre = dot(rows, up_w, ((1,), (0,)))
    sig = 1.0 / (1.0 + jnp.exp(-gate_pre))
    swish = gate_pre * sig
    grad_hidden = jnp.zeros_like(gate_pre)
    for i in range(0, depth, width):
        square = stack[2 * depth + i : 2 * depth + i + width]
        grad_hidden += dot(grads[:, i : i + width], square, ((1,), (1,)))
    grad_upre = (grad_hidden * swish).astype(jnp.bfloat16)
    grad_gpre = (grad_hidden * up_pre * sig * (1.0 + gate_pre * (1.0 - sig))).astype(jnp.bfloat16)
    back[...] = (dot(grad_gpre, gate_w, ((1,), (1,))) + dot(grad_upre, up_w, ((1,), (1,)))).astype(jnp.bfloat16)
    inner[0] = grad_gpre
    inner[1] = grad_upre
    inner[2] = (swish * up_pre).astype(jnp.bfloat16)


def expert_kernel(d, place, goals, stack, back, inner, case):
    me = lax.axis_index("group")
    lower = (me ^ d) > me
    full = jnp.max(place[:16, :128].astype(jnp.float32)) < EMPTY / 2
    sent = functools.reduce(jnp.logical_or, [goals[i] == (me ^ d) for i in range(goals.shape[0])])
    case[0] = jnp.where(full, jnp.where(lower, 1, 2), 0) + jnp.where(sent, jnp.where(lower, 2, 1), 0)

    @pl.when(full)
    def _():
        expert_pass(place, stack, back, inner)

    @pl.when(jnp.logical_not(full))
    def _():
        back[...] = jnp.zeros_like(back)
        inner[...] = jnp.zeros_like(inner)


def load_kernel(array, out, sem):
    copy = pltpu.make_async_copy(array, out, sem)
    copy.start()
    copy.wait()


def load(array):
    return pl.pallas_call(
        load_kernel,
        out_shape=VMEM(array.shape, array.dtype),
        in_specs=[spec(pl.ANY)],
        out_specs=spec(VMEM),
        scratch_shapes=[pltpu.SemaphoreType.DMA],
        compiler_params=params(),
        name="load",
    )(array)


def expert(d, place, goals, stack):
    block, depth = place.shape[0] // 2, place.shape[1]
    width = stack.shape[1]
    return pl.pallas_call(
        functools.partial(expert_kernel, d),
        out_shape=[
            jax.ShapeDtypeStruct((block, depth), jnp.bfloat16),
            jax.ShapeDtypeStruct((3, block, width), jnp.bfloat16),
            SMEM((1,), jnp.int32),
        ],
        in_specs=[spec(VMEM), spec(SMEM), spec(VMEM)],
        out_specs=[spec(VMEM), spec(VMEM), spec(SMEM)],
        compiler_params=params(),
        cost_estimate=pl.CostEstimate(
            flops=10 * block * depth * width, bytes_accessed=8 * depth * width, transcendentals=block * width
        ),
        name="expert",
    )(place, goals, stack)


def weights_kernel(count, *refs):
    places, inners = refs[:count], refs[count : 2 * count]
    grad_gate, grad_up, grad_down = refs[2 * count :]
    block = places[0].shape[0] // 2
    rows = jnp.concatenate([place[:block] for place in places], axis=0)
    grads = jnp.concatenate([place[block:] for place in places], axis=0)
    gpre, upre, hidden = (jnp.concatenate([inner[i] for inner in inners], axis=0) for i in range(3))
    grad_gate[0] = dot(rows, gpre, ((0,), (0,))).astype(jnp.bfloat16)
    grad_up[0] = dot(rows, upre, ((0,), (0,))).astype(jnp.bfloat16)
    grad_down[0] = dot(hidden, grads, ((0,), (0,))).astype(jnp.bfloat16)


def weights(places, inners):
    count = len(places)
    block, depth = places[0].shape[0] // 2, places[0].shape[1]
    width = inners[0].shape[2]
    tile = min(depth, 256)
    wide = jax.ShapeDtypeStruct((1, depth, width), jnp.bfloat16)
    tall = jax.ShapeDtypeStruct((1, width, depth), jnp.bfloat16)
    return pl.pallas_call(
        functools.partial(weights_kernel, count),
        out_shape=[wide, wide, tall],
        grid=(depth // tile,),
        in_specs=[pl.BlockSpec((2 * block, tile), lambda i: (0, i))] * count
        + [pl.BlockSpec((3, block, width), lambda i: (0, 0, 0))] * count,
        out_specs=[
            pl.BlockSpec((1, tile, width), lambda i: (0, i, 0)),
            pl.BlockSpec((1, tile, width), lambda i: (0, i, 0)),
            pl.BlockSpec((1, width, tile), lambda i: (0, 0, i)),
        ],
        compiler_params=params(),
        cost_estimate=pl.CostEstimate(
            flops=6 * count * block * depth * width, bytes_accessed=10 * depth * width, transcendentals=0
        ),
        name="weight_grads",
    )(*places, *inners)


def settle_kernel(hops, shape, goals, *refs):
    returned, out, empty, sems = refs[: len(hops)], refs[len(hops)], refs[len(hops) + 1], refs[len(hops) + 2]
    slots = shape[0]
    block = empty.shape[0]
    me = lax.axis_index("group")
    empty[...] = jnp.zeros_like(empty)
    for b in range(slots):
        target = out.at[pl.ds(b * block, block)]
        for hop, part in zip(hops, returned):

            @pl.when(goals[b] == hop(me))
            def _():
                pltpu.make_async_copy(part, target, sems.at[b]).start()

        @pl.when(goals[b] < 0)
        def _():
            pltpu.make_async_copy(empty, target, sems.at[b]).start()

    for b in range(slots):
        pltpu.make_async_copy(empty, out.at[pl.ds(b * block, block)], sems.at[b]).wait()


def combine_kernel(hops, shape, goals, *refs):
    returned, out, total = refs[: len(hops)], refs[len(hops)], refs[len(hops) + 1]
    slots, topk = shape
    block = out.shape[0] // slots
    me = lax.axis_index("group")
    for b in range(slots):
        total[...] = jnp.zeros_like(total)
        for k in range(topk):
            for hop, part in zip(hops, returned):

                @pl.when(goals[b * topk + k] == hop(me))
                def _():
                    total[...] += part[...].astype(jnp.float32)

        out[b * block : (b + 1) * block] = total[...].astype(jnp.bfloat16)


def combine(hops, shape, goals, returned):
    slots, topk = shape
    block, depth = returned[0].shape
    if topk == 1:
        kernel, where_from, where_to = settle_kernel, pl.ANY, pltpu.HBM
        scratch = [VMEM((block, depth), jnp.bfloat16), pltpu.SemaphoreType.DMA((slots,))]
    else:
        kernel, where_from, where_to = combine_kernel, VMEM, VMEM
        scratch = [VMEM((block, depth), jnp.float32)]
    return pl.pallas_call(
        functools.partial(kernel, hops, (slots, topk)),
        out_shape=where_to((slots * block, depth), jnp.bfloat16),
        in_specs=[spec(SMEM)] + [spec(where_from)] * len(hops),
        out_specs=spec(where_to),
        scratch_shapes=scratch,
        compiler_params=params(),
        name="combine",
    )(goals, *returned)


def xor_pairs(size, d):
    return [(i, i ^ d) for i in range(size)]


def to_xor(array, d, axis="group"):
    return lax.ppermute(array, axis, xor_pairs(lax.axis_size(axis), d))


def after(array, *others):
    return lax.optimization_barrier((array, *others))[0]


def give_back(case, back, d, beside=lambda: ()):
    pairs = xor_pairs(lax.axis_size("group"), d)
    up = [(a, b) for a, b in pairs if a < b]
    down = [(a, b) for a, b in pairs if a > b]

    def branch(perm):
        return lambda array: (lax.ppermute(array, "group", perm) if perm else array, beside())

    return lax.switch(case[0], [branch(perm) for perm in ([], up, down, pairs)], back)


def on_device(tokens, grad_out, router_gate, counts, routes, partner, w_gate, w_up, w_down):
    nodes, group = lax.axis_size("node"), lax.axis_size("group")
    shape = routes.shape[1:]
    order = sorted(range(1, group), key=lambda d: (d != 3, -d)) + [0]
    optional = (2,) if group == 4 else ()
    hops = [functools.partial(lambda d, me: me ^ d, d) for d in order]
    packed, plan, goals = pack(hops, partner, counts, routes, tokens, grad_out, router_gate)
    places = {d: to_xor(place, d) if d else place for d, place in zip(order, packed)}

    def move(d):
        return lambda *held: to_xor(stacked(*held), d, "node")

    stack = load(lax.switch(plan[0], [move(d) for d in range(1, nodes)], w_gate, w_up, w_down))
    inners, returned = {}, {}
    turns = [d for d in (3, 1, 0) if d < group] + [2] + list(range(4, group))
    for d in turns:
        back, inners[d], case = expert(d, places[d], goals, stack)
        stack = after(stack, inners[d])
        if d == 0 or d not in optional:
            returned[d] = to_xor(back, d) if d else back
        elif d != optional[-1]:
            returned[d], _ = give_back(case, back, d)
            stack = after(stack, returned[d])
        else:
            beside = lambda: weights([places[d] for d in order], [inners[d] for d in order])
            returned[d], grads = give_back(case, back, d, beside)
    if not optional:
        grads = weights([places[d] for d in order], [inners[d] for d in order])
    return (combine(hops, shape, goals, [returned[d] for d in order]), *grads)


def solution(mesh):
    both = ("node", "group")
    rows = P(both, None)
    cube = P(both, None, None)
    return jax.shard_map(
        on_device,
        mesh=mesh,
        in_specs=(rows, rows, rows, P(both), cube, P(), cube, cube, cube),
        out_specs=(rows, cube, cube, cube),
        check_vma=False,
    )
```

```python
import functools

import jax
import jax.numpy as jnp
from jax import lax
from jax.experimental import pallas as pl
from jax.experimental.pallas import tpu as pltpu
from jax.sharding import PartitionSpec as P

VMEM = pltpu.VMEM
SMEM = pltpu.SMEM
LIMIT = 48 * 1024 * 1024


def dot(left, right, dims):
    return lax.dot_general(left, right, (dims, ((), ())), preferred_element_type=jnp.float32)


def params():
    return pltpu.CompilerParams(vmem_limit_bytes=LIMIT)


def in_hbm(array):
    return pltpu.with_memory_space_constraint(array, pltpu.HBM)


def spec(space):
    return pl.BlockSpec(memory_space=space)


EMPTY = 64.0


def pack_kernel(hops, shape, counts, partner, routes, tokens, grad_out, gate, *refs):
    slots, topk = shape
    places, (plan, goals) = refs[: len(hops)], refs[len(hops) : len(hops) + 2]
    partner_s, routes_s, tokens_v, grads_v, gate_v, sems = refs[len(hops) + 2 :]
    copies = [
        pltpu.make_async_copy(source, target, sems.at[i])
        for i, (source, target) in enumerate(
            [(routes, routes_s), (partner, partner_s), (gate, gate_v), (grad_out, grads_v), (tokens, tokens_v)]
        )
    ]
    for copy in copies:
        copy.start()
    block = grads_v.shape[0] // slots
    me, node = lax.axis_index("group"), lax.axis_index("node")
    copies[0].wait()
    entries = [(b, k) for b in range(slots) for k in range(topk)]
    sent = [[(routes_s[b * topk + k] == hop(me)) & (b < counts[0]) for b, k in entries] for hop in hops]
    for i, place in enumerate(places):

        @pl.when(jnp.logical_not(functools.reduce(jnp.logical_or, sent[i])))
        def _():
            place[...] = jnp.full(place.shape, EMPTY, place.dtype)

    for copy in copies[1:]:
        copy.wait()
    plan[0] = (node ^ partner_s[node]) - 1
    for i, (b, _) in enumerate(entries):
        goals[i] = jnp.where(b < counts[0], routes_s[i], -1)
    for i, place in enumerate(places):
        for (b, k), found in zip(entries, sent[i]):

            @pl.when(found)
            def _():
                rows = pl.ds(b * block, block)
                scaled = gate_v[k : k + 1, rows].T * grads_v[rows].astype(jnp.float32)
                place[:block] = tokens_v[rows]
                place[block:] = scaled.astype(jnp.bfloat16)


def pack(hops, partner, counts, routes, tokens, grad_out, gate):
    slots, topk = routes.shape[1], routes.shape[2]
    length, depth = tokens.shape
    place = jax.ShapeDtypeStruct((2 * length // slots, depth), jnp.bfloat16)
    *places, plan, goals = pl.pallas_call(
        functools.partial(pack_kernel, hops, (slots, topk)),
        out_shape=[place] * len(hops) + [SMEM((1,), jnp.int32), SMEM((slots * topk,), jnp.int32)],
        in_specs=[spec(SMEM)] + [spec(pltpu.HBM)] * 5,
        out_specs=[spec(VMEM)] * len(hops) + [spec(SMEM)] * 2,
        scratch_shapes=[
            SMEM(partner.shape, jnp.int32),
            SMEM((slots * topk,), jnp.int32),
            VMEM((length, depth), jnp.bfloat16),
            VMEM((length, depth), jnp.bfloat16),
            VMEM((topk, length), jnp.float32),
            pltpu.SemaphoreType.DMA((5,)),
        ],
        compiler_params=params(),
        name="pack",
    )(counts, *map(in_hbm, (partner, routes.reshape(slots * topk), tokens, grad_out, gate.T)))
    return places, plan, goals


def stack_kernel(w_gate, w_up, w_down, stack, sems):
    depth, width = w_gate.shape[1:]
    copies = [
        pltpu.make_async_copy(w_gate.at[0], stack.at[pl.ds(0, depth)], sems.at[0]),
        pltpu.make_async_copy(w_up.at[0], stack.at[pl.ds(depth, depth)], sems.at[1]),
    ] + [
        pltpu.make_async_copy(
            w_down.at[0, :, pl.ds(i * width, width)],
            stack.at[pl.ds(2 * depth + i * width, width)],
            sems.at[2 + i],
        )
        for i in range(depth // width)
    ]
    for copy in copies:
        copy.start()
    for copy in copies:
        copy.wait()


def stacked(w_gate, w_up, w_down):
    depth, width = w_gate.shape[1:]
    return pl.pallas_call(
        stack_kernel,
        out_shape=jax.ShapeDtypeStruct((3 * depth, width), jnp.bfloat16),
        in_specs=[spec(pltpu.HBM)] * 3,
        out_specs=spec(VMEM),
        scratch_shapes=[pltpu.SemaphoreType.DMA((2 + depth // width,))],
        compiler_params=params(),
        name="stack",
    )(*map(in_hbm, (w_gate, w_up, w_down)))


def expert_pass(place, stack, back, inner):
    block, depth = place.shape[0] // 2, place.shape[1]
    width = stack.shape[1]
    rows, grads = place[:block], place[block:]
    gate_w, up_w = stack[:depth], stack[depth : 2 * depth]
    gate_pre = dot(rows, gate_w, ((1,), (0,)))
    up_pre = dot(rows, up_w, ((1,), (0,)))
    sig = 1.0 / (1.0 + jnp.exp(-gate_pre))
    swish = gate_pre * sig
    grad_hidden = jnp.zeros_like(gate_pre)
    for i in range(0, depth, width):
        square = stack[2 * depth + i : 2 * depth + i + width]
        grad_hidden += dot(grads[:, i : i + width], square, ((1,), (1,)))
    grad_upre = (grad_hidden * swish).astype(jnp.bfloat16)
    grad_gpre = (grad_hidden * up_pre * sig * (1.0 + gate_pre * (1.0 - sig))).astype(jnp.bfloat16)
    back[...] = (dot(grad_gpre, gate_w, ((1,), (1,))) + dot(grad_upre, up_w, ((1,), (1,)))).astype(jnp.bfloat16)
    inner[0] = grad_gpre
    inner[1] = grad_upre
    inner[2] = (swish * up_pre).astype(jnp.bfloat16)


def expert_kernel(d, place, goals, stack, back, inner, case):
    me = lax.axis_index("group")
    lower = (me ^ d) > me
    full = jnp.max(place[:16, :128].astype(jnp.float32)) < EMPTY / 2
    sent = functools.reduce(jnp.logical_or, [goals[i] == (me ^ d) for i in range(goals.shape[0])])
    case[0] = jnp.where(full, jnp.where(lower, 1, 2), 0) + jnp.where(sent, jnp.where(lower, 2, 1), 0)

    @pl.when(full)
    def _():
        expert_pass(place, stack, back, inner)

    @pl.when(jnp.logical_not(full))
    def _():
        back[...] = jnp.zeros_like(back)
        inner[...] = jnp.zeros_like(inner)


def load_kernel(array, out, sem):
    copy = pltpu.make_async_copy(array, out, sem)
    copy.start()
    copy.wait()


def load(array):
    return pl.pallas_call(
        load_kernel,
        out_shape=VMEM(array.shape, array.dtype),
        in_specs=[spec(pl.ANY)],
        out_specs=spec(VMEM),
        scratch_shapes=[pltpu.SemaphoreType.DMA],
        compiler_params=params(),
        name="load",
    )(array)


def expert(d, place, goals, stack):
    block, depth = place.shape[0] // 2, place.shape[1]
    width = stack.shape[1]
    return pl.pallas_call(
        functools.partial(expert_kernel, d),
        out_shape=[
            jax.ShapeDtypeStruct((block, depth), jnp.bfloat16),
            jax.ShapeDtypeStruct((3, block, width), jnp.bfloat16),
            SMEM((1,), jnp.int32),
        ],
        in_specs=[spec(VMEM), spec(SMEM), spec(VMEM)],
        out_specs=[spec(VMEM), spec(VMEM), spec(SMEM)],
        compiler_params=params(),
        cost_estimate=pl.CostEstimate(
            flops=10 * block * depth * width, bytes_accessed=8 * depth * width, transcendentals=block * width
        ),
        name="expert",
    )(place, goals, stack)


def weights_kernel(count, *refs):
    places, inners = refs[:count], refs[count : 2 * count]
    grad_gate, grad_up, grad_down = refs[2 * count :]
    block = places[0].shape[0] // 2
    rows = jnp.concatenate([place[:block] for place in places], axis=0)
    grads = jnp.concatenate([place[block:] for place in places], axis=0)
    gpre, upre, hidden = (jnp.concatenate([inner[i] for inner in inners], axis=0) for i in range(3))
    grad_gate[0] = dot(rows, gpre, ((0,), (0,))).astype(jnp.bfloat16)
    grad_up[0] = dot(rows, upre, ((0,), (0,))).astype(jnp.bfloat16)
    grad_down[0] = dot(hidden, grads, ((0,), (0,))).astype(jnp.bfloat16)


def weights(places, inners):
    count = len(places)
    block, depth = places[0].shape[0] // 2, places[0].shape[1]
    width = inners[0].shape[2]
    tile = min(depth, 512)
    wide = jax.ShapeDtypeStruct((1, depth, width), jnp.bfloat16)
    tall = jax.ShapeDtypeStruct((1, width, depth), jnp.bfloat16)
    return pl.pallas_call(
        functools.partial(weights_kernel, count),
        out_shape=[wide, wide, tall],
        grid=(depth // tile,),
        in_specs=[pl.BlockSpec((2 * block, tile), lambda i: (0, i))] * count
        + [pl.BlockSpec((3, block, width), lambda i: (0, 0, 0))] * count,
        out_specs=[
            pl.BlockSpec((1, tile, width), lambda i: (0, i, 0)),
            pl.BlockSpec((1, tile, width), lambda i: (0, i, 0)),
            pl.BlockSpec((1, width, tile), lambda i: (0, 0, i)),
        ],
        compiler_params=params(),
        cost_estimate=pl.CostEstimate(
            flops=6 * count * block * depth * width, bytes_accessed=10 * depth * width, transcendentals=0
        ),
        name="weight_grads",
    )(*places, *inners)


def settle_kernel(hops, shape, goals, *refs):
    returned, out, empty, sems = refs[: len(hops)], refs[len(hops)], refs[len(hops) + 1], refs[len(hops) + 2]
    slots = shape[0]
    block = empty.shape[0]
    me = lax.axis_index("group")
    empty[...] = jnp.zeros_like(empty)
    for b in range(slots):
        target = out.at[pl.ds(b * block, block)]
        for hop, part in zip(hops, returned):

            @pl.when(goals[b] == hop(me))
            def _():
                pltpu.make_async_copy(part, target, sems.at[b]).start()

        @pl.when(goals[b] < 0)
        def _():
            pltpu.make_async_copy(empty, target, sems.at[b]).start()

    for b in range(slots):
        pltpu.make_async_copy(empty, out.at[pl.ds(b * block, block)], sems.at[b]).wait()


def combine_kernel(hops, shape, goals, *refs):
    returned, out, total = refs[: len(hops)], refs[len(hops)], refs[len(hops) + 1]
    slots, topk = shape
    block = out.shape[0] // slots
    me = lax.axis_index("group")
    for b in range(slots):
        total[...] = jnp.zeros_like(total)
        for k in range(topk):
            for hop, part in zip(hops, returned):

                @pl.when(goals[b * topk + k] == hop(me))
                def _():
                    total[...] += part[...].astype(jnp.float32)

        out[b * block : (b + 1) * block] = total[...].astype(jnp.bfloat16)


def combine(hops, shape, goals, returned):
    slots, topk = shape
    block, depth = returned[0].shape
    if topk == 1:
        kernel, where_from, where_to = settle_kernel, pl.ANY, pltpu.HBM
        scratch = [VMEM((block, depth), jnp.bfloat16), pltpu.SemaphoreType.DMA((slots,))]
    else:
        kernel, where_from, where_to = combine_kernel, VMEM, VMEM
        scratch = [VMEM((block, depth), jnp.float32)]
    return pl.pallas_call(
        functools.partial(kernel, hops, (slots, topk)),
        out_shape=where_to((slots * block, depth), jnp.bfloat16),
        in_specs=[spec(SMEM)] + [spec(where_from)] * len(hops),
        out_specs=spec(where_to),
        scratch_shapes=scratch,
        compiler_params=params(),
        name="combine",
    )(goals, *returned)


def xor_pairs(size, d):
    return [(i, i ^ d) for i in range(size)]


def to_xor(array, d, axis="group"):
    return lax.ppermute(array, axis, xor_pairs(lax.axis_size(axis), d))


def after(array, *others):
    return lax.optimization_barrier((array, *others))[0]


def give_back(case, back, d, beside=lambda: ()):
    pairs = xor_pairs(lax.axis_size("group"), d)
    up = [(a, b) for a, b in pairs if a < b]
    down = [(a, b) for a, b in pairs if a > b]

    def branch(perm):
        return lambda array: (lax.ppermute(array, "group", perm) if perm else array, beside())

    return lax.switch(case[0], [branch(perm) for perm in ([], up, down, pairs)], back)


def on_device(tokens, grad_out, router_gate, counts, routes, partner, w_gate, w_up, w_down):
    nodes, group = lax.axis_size("node"), lax.axis_size("group")
    shape = routes.shape[1:]
    order = sorted(range(1, group), key=lambda d: (d != 3, -d)) + [0]
    optional = (2,) if group == 4 else ()
    hops = [functools.partial(lambda d, me: me ^ d, d) for d in order]
    packed, plan, goals = pack(hops, partner, counts, routes, tokens, grad_out, router_gate)
    places = {d: to_xor(place, d) if d else place for d, place in zip(order, packed)}

    def move(d):
        return lambda *held: to_xor(stacked(*held), d, "node")

    stack = load(lax.switch(plan[0], [move(d) for d in range(1, nodes)], w_gate, w_up, w_down))
    inners, returned = {}, {}
    turns = [d for d in (3, 0, 1) if d < group] + [2] + list(range(4, group))
    for d in turns:
        back, inners[d], case = expert(d, places[d], goals, stack)
        stack = after(stack, inners[d])
        if d == 0 or d not in optional:
            returned[d] = to_xor(back, d) if d else back
        elif d != optional[-1]:
            returned[d], _ = give_back(case, back, d)
            stack = after(stack, returned[d])
        else:
            beside = lambda: weights([places[d] for d in order], [inners[d] for d in order])
            returned[d], grads = give_back(case, back, d, beside)
    if not optional:
        grads = weights([places[d] for d in order], [inners[d] for d in order])
    return (combine(hops, shape, goals, [returned[d] for d in order]), *grads)


def solution(mesh):
    both = ("node", "group")
    rows = P(both, None)
    cube = P(both, None, None)
    return jax.shard_map(
        on_device,
        mesh=mesh,
        in_specs=(rows, rows, rows, P(both), cube, P(), cube, cube, cube),
        out_specs=(rows, cube, cube, cube),
        check_vma=False,
    )
```
